32 devices in a mesh: seg: 2 (over x), seq: 16 (over z, y, core).
Axes of the slice: x: 2, y: 2, z: 4, core: 2. Of those that a mesh axis runs over, the one named last changes fastest.
Arguments:
- tokens: bfloat16 [2, 2, 8192, 512], P(None, 'seg', 'seq'), may hold values from -6 to 6
- lengths: int32 [2, 2, 96], replicated, may hold values from 0 to 512, as said below
- qkv_weight: bfloat16 [512, 1536], replicated, may hold values from -0.25 to 0.25
- query_bias: bfloat16 [512], replicated, may hold values from -3 to 3
- value_bias: bfloat16 [512], replicated, may hold values from -3 to 3
- out_weight: bfloat16 [512, 512], replicated, may hold values from -1 to 1
- out_bias: bfloat16 [512], replicated, may hold values from -3 to 3
- attn_gain: bfloat16 [512], replicated, may hold values from 0.5 to 1.5
- attn_shift: bfloat16 [512], replicated, may hold values from -3 to 3
- up_weight: bfloat16 [512, 2048], replicated, may hold values from -0.25 to 0.25
- up_bias: bfloat16 [2048], replicated, may hold values from -3 to 3
- down_weight: bfloat16 [2048, 512], replicated, may hold values from -0.125 to 0.125
- down_bias: bfloat16 [512], replicated, may hold values from -3 to 3
- ffn_gain: bfloat16 [512], replicated, may hold values from 0.5 to 1.5
- ffn_shift: bfloat16 [512], replicated, may hold values from -3 to 3
- cotangent: bfloat16 [2, 2, 8192, 512], P(None, 'seg', 'seq'), may hold values from -6 to 6
Outputs:
- output: bfloat16 [2, 2, 8192, 512], P(None, 'seg', 'seq')
- tokens_grad: float32 [2, 2, 8192, 512], P(None, 'seg', 'seq')
- qkv_weight_grad: float32 [512, 1536], replicated
- query_bias_grad: float32 [512], replicated
- value_bias_grad: float32 [512], replicated
- out_weight_grad: float32 [512, 512], replicated
- out_bias_grad: float32 [512], replicated
- attn_gain_grad: float32 [512], replicated
- attn_shift_grad: float32 [512], replicated
- up_weight_grad: float32 [512, 2048], replicated
- up_bias_grad: float32 [2048], replicated
- down_weight_grad: float32 [2048, 512], replicated
- down_bias_grad: float32 [512], replicated
- ffn_gain_grad: float32 [512], replicated
- ffn_shift_grad: float32 [512], replicated
The draws below stay inside these ranges and needn't reach their ends.
Inputs may be any that keep to these rules, and one draw needn't show every extreme that they name: `lengths`: A pair spans max of its two counts in slots; spans lie end to end from the first slot in pair order, the same in both segments; no span exceeds 512 and one span of every micro-batch is exactly 512; the shorter count of a pair is at least min(span, 10); the last spans may be cut or empty at the segment's end.
All inputs are finite; a program needn't handle non-finite values.
Results may differ from the reference program's by a relative error of at most 0.014.
Values may be sent and summed in bfloat16 or wider, within the bound.
No kernel may reach another device: no remote copies, remote signals or barrier semaphores. Data moves between devices by JAX's collectives and lax.ppermute only.
A program may use at most 384 MiB of HBM per device.

```python
import math
import jax
import jax.numpy as jnp
from jax import lax

D = 512
HEADS = 8
HEAD_DIM = 64
FF = 2048
MICRO = 2
LONGEST = 512
SHORTEST = 10
SLOTS = 8192
PAIRS = 96


def draw_pairs(key):
    key_levels, key_extra, key_chosen, key_other, key_side = jax.random.split(key, 5)
    levels = jax.random.randint(key_levels, (PAIRS,), 0, 7)
    unit_len = max(1, LONGEST // 64)
    reach_len = unit_len * jnp.power(jnp.int32(2), levels)
    extra_len = jax.random.randint(key_extra, (PAIRS,), 0, reach_len + 1)
    pair_spans = jnp.minimum(SHORTEST + extra_len, LONGEST).astype(jnp.int32)
    chosen = jax.random.randint(key_chosen, (), 0, max(1, PAIRS // 8))
    pair_spans = jnp.where(jnp.arange(PAIRS, dtype=jnp.int32) == chosen, LONGEST, pair_spans).astype(jnp.int32)
    pair_ends = jnp.cumsum(pair_spans).astype(jnp.int32)
    pair_starts = pair_ends - pair_spans
    pair_spans = jnp.clip(SLOTS - pair_starts, 0, pair_spans).astype(jnp.int32)
    shorter = jnp.minimum(pair_spans, SHORTEST)
    offsets = jax.random.randint(key_other, (PAIRS,), 0, LONGEST + 1)
    other_len = pair_spans - offsets % (pair_spans - shorter + 1)
    side_pick = jax.random.randint(key_side, (PAIRS,), 0, 2)
    premise = jnp.where(side_pick == 0, pair_spans, other_len)
    hypothesis = jnp.where(side_pick == 0, other_len, pair_spans)
    return jnp.stack([premise, hypothesis]).astype(jnp.int32)


def draw_lengths(key, part):
    return jnp.stack([draw_pairs(jax.random.fold_in(key, micro_idx)) for micro_idx in range(MICRO)])


def level_of(key, shape, cuts, low, top_value):
    def one(dim, parts):
        draws = jax.random.uniform(jax.random.fold_in(jax.random.fold_in(key, 6), dim), (parts,), jnp.float32, low / len(cuts), top_value / len(cuts))
        return jnp.repeat(jnp.exp(draws), shape[dim] // parts).reshape((-1,) + (1,) * (len(shape) - dim - 1))

    level = one(*cuts[0])
    for cut in cuts[1:]:
        level = level * one(*cut)
    return level


def noise(rng, extent, scale, bound, shards=(), kind=jnp.bfloat16):
    array = scale * jax.random.normal(rng, extent, jnp.float32)
    if shards:
        array = array * level_of(rng, extent, shards, -0.22, 0.18)
    return jnp.clip(array, -bound, bound).astype(kind)


def setup_inputs(seed: int = 0) -> dict:
    arg_keys = jax.random.split(jax.random.key(seed), 17)
    return {
        "tokens": noise(arg_keys[0], (MICRO, 2, SLOTS, D), 1.0, 6.0, ((1, 2), (2, 16))),
        "lengths": draw_lengths(jax.random.fold_in(arg_keys[16], 71), 0),
        "qkv_weight": noise(arg_keys[2], (D, 3 * D), D ** -0.5, 0.25),
        "query_bias": noise(arg_keys[3], (D,), 0.5, 3.0),
        "value_bias": noise(arg_keys[4], (D,), 0.5, 3.0),
        "out_weight": noise(arg_keys[5], (D, D), (D // 16) ** -0.5, 1.0),
        "out_bias": noise(arg_keys[6], (D,), 0.5, 3.0),
        "attn_gain": jnp.clip(1.0 + 0.1 * jax.random.normal(arg_keys[7], (D,), jnp.float32), 0.5, 1.5).astype(jnp.bfloat16),
        "attn_shift": noise(arg_keys[8], (D,), 0.5, 3.0),
        "up_weight": noise(arg_keys[9], (D, FF), D ** -0.5, 0.25),
        "up_bias": noise(arg_keys[10], (FF,), 0.5, 3.0),
        "down_weight": noise(arg_keys[11], (FF, D), FF ** -0.5, 0.125),
        "down_bias": noise(arg_keys[12], (D,), 0.5, 3.0),
        "ffn_gain": jnp.clip(1.0 + 0.1 * jax.random.normal(arg_keys[13], (D,), jnp.float32), 0.5, 1.5).astype(jnp.bfloat16),
        "ffn_shift": noise(arg_keys[14], (D,), 0.5, 3.0),
        "cotangent": noise(arg_keys[15], (MICRO, 2, SLOTS, D), 1.0, 6.0, ((1, 2), (2, 16))),
    }


@jax.custom_vjp
def low(v):
    return lax.optimization_barrier(v.astype(jnp.bfloat16)).astype(jnp.float32)

@jax.custom_vjp
def low_back(v):
    return v

def low_keep(v):
    return (low(v), None)

def low_pass(kept, grad):
    return (grad,)

def back_keep(v):
    return (v, None)

def back_low(kept, grad):
    return (low(grad),)
low.defvjp(low_keep, low_pass)
low_back.defvjp(back_keep, back_low)
NEG_BIG = -1e+30
FLOOR_MAX = -10000.0
EPS = 1e-12
PRECISE = lax.Precision.HIGHEST

def matmul(left, right):
    return jnp.dot(left, right, precision=PRECISE, preferred_element_type=jnp.float32)

def layer_norm(hidden, gain_vec, shift_vec):
    mean_val = lax.optimization_barrier(jnp.mean(hidden, axis=-1, keepdims=True))
    centred = hidden - mean_val
    var_val = lax.optimization_barrier(jnp.mean(centred * centred, axis=-1, keepdims=True))
    return centred * lax.rsqrt(var_val + EPS) * gain_vec + shift_vec

def gelu_exact(values):
    return jax.nn.gelu(values, approximate=False)

def pair_table(positions, lens_pair):
    pair_spans = jnp.maximum(lens_pair[0], lens_pair[1])
    pair_ends = jnp.cumsum(pair_spans).astype(jnp.int32)
    pair_starts = pair_ends - pair_spans
    inside = (pair_starts[None, :] <= positions[:, None]) & (positions[:, None] < pair_ends[None, :])
    offset = positions[:, None] - pair_starts[None, :]
    labels = jnp.arange(pair_spans.shape[0], dtype=jnp.int32)
    pair_id = lax.optimization_barrier(jnp.sum(jnp.where(inside, labels[None, :], 0), axis=1)).astype(jnp.int32)
    pair_id = jnp.where(jnp.any(inside, axis=1), pair_id, -1)
    valid_first = jnp.any(inside & (offset < lens_pair[0][None, :]), axis=1)
    valid_second = jnp.any(inside & (offset < lens_pair[1][None, :]), axis=1)
    return (pair_id, valid_first, valid_second)

def micro_layer(tokens_f, lens_pair, qkv_weight, query_bias, value_bias, out_weight, out_bias, attn_gain, attn_shift, up_weight, up_bias, down_weight, down_bias, ffn_gain, ffn_shift):
    model_width = tokens_f.shape[-1]
    slot_count = tokens_f.shape[1]
    row_block = math.gcd(2 * slot_count, 4096)
    slabs = tokens_f.reshape(-1, row_block, model_width)

    def project(row_slab):
        lin_qkv = low_back(matmul(row_slab, qkv_weight))
        query = low(lin_qkv[:, :model_width] + query_bias)
        key_part = low(lin_qkv[:, model_width:2 * model_width])
        value_part = low(lin_qkv[:, 2 * model_width:] + value_bias)
        return (query, key_part, value_part)
    queries, keys_all, values_all = lax.map(jax.checkpoint(project), slabs)
    queries = queries.reshape(2, slot_count, HEADS, HEAD_DIM)
    keys_all = keys_all.reshape(2, slot_count, model_width)
    values_all = values_all.reshape(2, slot_count, model_width)
    margin = LONGEST
    query_block = math.gcd(slot_count, 512)
    block_count = slot_count // query_block
    window = query_block + 2 * margin
    key_pad = jnp.pad(keys_all, ((0, 0), (margin, margin), (0, 0)))
    value_pad = jnp.pad(values_all, ((0, 0), (margin, margin), (0, 0)))
    positions = jnp.arange(-margin, slot_count + margin, dtype=jnp.int32)
    pair_ids, valid_first, valid_second = pair_table(positions, lens_pair)
    key_valid = jnp.stack([valid_first, valid_second])
    query_pair = pair_ids[margin:margin + slot_count]
    score_scale = 1.0 / math.sqrt(HEAD_DIM)

    def attend(block_idx):
        segment_idx = (block_idx // block_count).astype(jnp.int32)
        start_row = (block_idx % block_count * query_block).astype(jnp.int32)
        zero_idx = jnp.int32(0)
        q_here = lax.dynamic_slice(queries, (segment_idx, start_row, zero_idx, zero_idx), (1, query_block, HEADS, HEAD_DIM))[0]
        k_here = lax.dynamic_slice(key_pad, (zero_idx, start_row, zero_idx), (2, window, model_width)).reshape(2 * window, HEADS, HEAD_DIM)
        v_here = lax.dynamic_slice(value_pad, (zero_idx, start_row, zero_idx), (2, window, model_width)).reshape(2 * window, HEADS, HEAD_DIM)
        pair_here = lax.dynamic_slice(query_pair, (start_row,), (query_block,))
        key_pair_here = lax.dynamic_slice(pair_ids, (start_row,), (window,))
        key_valid_here = lax.dynamic_slice(key_valid, (zero_idx, start_row), (2, window)).reshape(-1)
        allowed = (pair_here[:, None] == jnp.concatenate([key_pair_here, key_pair_here])[None, :]) & key_valid_here[None, :]
        raw = jnp.einsum('qhd,khd->hqk', q_here, k_here, precision=PRECISE)
        scores = low_back(raw * score_scale)
        masked = jnp.where(allowed[None], scores, NEG_BIG)
        row_max = jnp.maximum(lax.optimization_barrier(jnp.max(masked, axis=-1, keepdims=True)), FLOOR_MAX)
        expd = jnp.exp(masked - row_max)
        row_total = lax.optimization_barrier(jnp.sum(expd, axis=-1, keepdims=True))
        probs = expd / jnp.maximum(row_total, 1.0)
        context = jnp.einsum('hqk,khd->qhd', low(probs), v_here, precision=PRECISE)
        return low(low_back(context.reshape(query_block, model_width)))
    contexts = lax.map(jax.checkpoint(attend), jnp.arange(2 * block_count, dtype=jnp.int32))
    contexts = contexts.reshape(-1, row_block, model_width)

    def finish(slab_pair):
        row_in, ctx_in = slab_pair
        attn_out = low_back(matmul(ctx_in, out_weight)) + out_bias
        normed = layer_norm(row_in + attn_out, attn_gain, attn_shift)
        pre_act = low_back(matmul(low(normed), up_weight) + up_bias)
        act_val = low(gelu_exact(pre_act))
        down_out = low_back(matmul(act_val, down_weight)) + down_bias
        return layer_norm(normed + down_out, ffn_gain, ffn_shift)
    result = lax.map(jax.checkpoint(finish), (slabs, contexts))
    return result.reshape(2, slot_count, model_width)

def reference(tokens, lengths, qkv_weight, query_bias, value_bias, out_weight, out_bias, attn_gain, attn_shift, up_weight, up_bias, down_weight, down_bias, ffn_gain, ffn_shift, cotangent):
    params = tuple((item.astype(jnp.float32) for item in (qkv_weight, query_bias, value_bias, out_weight, out_bias, attn_gain, attn_shift, up_weight, up_bias, down_weight, down_bias, ffn_gain, ffn_shift)))
    grad_sums = [jnp.zeros(item.shape, jnp.float32) for item in params]
    outputs = []
    input_grads = []
    for micro_idx in range(MICRO):
        lens_pair = lengths[micro_idx]

        def forward(tokens_f, *weights):
            return micro_layer(tokens_f, lens_pair, *weights)
        result, pullback = jax.vjp(forward, tokens[micro_idx].astype(jnp.float32), *params)
        grads_all = pullback(cotangent[micro_idx].astype(jnp.float32))
        outputs.append(result.astype(jnp.bfloat16))
        input_grads.append(grads_all[0])
        grad_sums = [prior + update for prior, update in zip(grad_sums, grads_all[1:])]
    return (jnp.stack(outputs), jnp.stack(input_grads), grad_sums[0], grad_sums[1], grad_sums[2], grad_sums[3], grad_sums[4], grad_sums[5], grad_sums[6], grad_sums[7], grad_sums[8], grad_sums[9], grad_sums[10], grad_sums[11], grad_sums[12])
```

```python
import functools
import math

import jax
import jax.numpy as jnp
from jax import lax
from jax.experimental import pallas as pl
from jax.experimental.pallas import tpu as pltpu
from jax.sharding import PartitionSpec as P

HEADS = 8
HEAD_DIM = 64
LONGEST = 512
FLOOR_MAX = -10000.0
MASK_OFF = -1e30
EPS = 1e-12
LANES = 128
SLOT_TILE = 128
DIGIT = 13
DIGITS = 3
BAD_LANE = DIGIT * DIGITS
STAT_LANE = BAD_LANE + 1
GROUP = HEADS // 2
WIDE = GROUP * HEAD_DIM
PAIRED = WIDE // LANES
CHAIN_ROWS = 256
BF = jnp.bfloat16
F32 = jnp.float32
ANY = pl.BlockSpec(memory_space=pl.ANY)
SMEM = pl.BlockSpec(memory_space=pltpu.SMEM)


def whole(shape):
    zeros = (0,) * len(shape)
    return pl.BlockSpec(shape, lambda _: zeros)


def row_block(rows, cols):
    return pl.BlockSpec((rows, cols), lambda i: (i, 0))


def vmem(mega):
    return pltpu.CompilerParams(vmem_limit_bytes=mega * 1024 * 1024)


def cost(giga, mega):
    return pl.CostEstimate(
        flops=int(giga * 10**9), bytes_accessed=int(mega * 10**6), transcendentals=0
    )


def dot_nn(left, right):
    return lax.dot_general(left, right, (((1,), (0,)), ((), ())), preferred_element_type=F32)


def dot_nt(left, right):
    return lax.dot_general(left, right, (((1,), (1,)), ((), ())), preferred_element_type=F32)


def dot_tn(left, right):
    return lax.dot_general(left, right, (((0,), (0,)), ((), ())), preferred_element_type=F32)


def lanes_of(rows):
    return lax.broadcasted_iota(jnp.int32, (rows, LANES), 1)


def in_head(head, rows):
    lane = lanes_of(rows)
    return lane < HEAD_DIM if head % 2 == 0 else lane >= HEAD_DIM


def stat_lane(head):
    return STAT_LANE + 3 * head + (HEAD_DIM if head % 2 == 0 else 0)


def ones_row(head, rows):
    lane = lanes_of(rows)
    first = stat_lane(head)
    return ((lane >= first) & (lane < first + 3)).astype(F32).astype(BF)


def pair_cols(part, head):
    first = part * WIDE + (head // 2) * LANES
    return slice(first, first + LANES)


def both(ref, start, cols):
    return jnp.concatenate(
        [ref[seg, pl.ds(start, SLOT_TILE), cols] for seg in range(2)], axis=0
    )


def three_parts(values):
    high = values.astype(BF).astype(F32)
    rest = values - high
    mid = rest.astype(BF).astype(F32)
    low = (rest - mid).astype(BF).astype(F32)
    return high, mid, low


def copy_all(copies):
    for item in copies:
        item.start()
    for item in copies:
        item.wait()


def block_copies(blocks, scratch, sems, first):
    rows = scratch.shape[1] // 3
    return [
        pltpu.make_async_copy(
            block, scratch.at[:, pl.ds(at * rows, rows), :], sems.at[first + at]
        )
        for at, block in enumerate(blocks)
    ]


def slot_start(tile):
    return pl.multiple_of(tile * SLOT_TILE, SLOT_TILE)


def query_codes(fq, start, level=None):
    codes = fq[pl.ds(start, SLOT_TILE), :]
    codes = jnp.concatenate([codes, codes], axis=0)
    return codes if level is None else codes + level


def spread_stats(stats):
    wide = stats.astype(F32)
    rolled = pltpu.roll(wide, HEAD_DIM, 1)
    lower = lanes_of(stats.shape[0]) < HEAD_DIM
    level = jnp.where(lower, wide, rolled)
    delta = jnp.where(lower, rolled, wide)
    return level.astype(BF), delta.astype(BF)


def staged(items, begin, finish, ahead=2):
    held = []
    for item in items:
        held.append((item, begin(item)))
        if len(held) > ahead:
            finish(*held.pop(0))
    for entry in held:
        finish(*entry)


def projector(tok, lin, weights, bias):
    rows = 2 * SLOT_TILE

    def project(tile, carry):
        start = slot_start(tile)
        cells = dot_nn(both(tok, start, slice(0, tok.shape[2])), weights[...])
        cells = (cells + bias[0:1, :]).astype(BF)
        for part in range(3):
            cols = slice(part * WIDE, (part + 1) * WIDE)
            piece = cells[:, cols]
            if part == 0:
                piece = piece * (1.0 / math.sqrt(HEAD_DIM))
            for seg in range(2):
                lin[seg, pl.ds(start, SLOT_TILE), cols] = piece[
                    seg * SLOT_TILE : (seg + 1) * SLOT_TILE
                ]
        return carry

    return project


def make_queries(qa, lin, start, codes):
    rows = 2 * SLOT_TILE
    for head in range(GROUP):
        qa[head] = jnp.where(in_head(head, rows), both(lin, start, pair_cols(0, head)), codes)


def attend_step(qa, peak, acc, lin, start, code):
    rows = 2 * SLOT_TILE

    def begin(head):
        keys = both(lin, start, pair_cols(1, head))
        keys = jnp.where(in_head(head, rows), keys, code)
        return dot_nt(qa[head], keys)

    def finish(head, scores):
        vals = both(lin, start, pair_cols(2, head))
        vals = jnp.where(in_head(head, rows), vals, ones_row(head, rows))
        before = peak[head]
        top = jnp.maximum(before, jnp.max(scores, axis=1, keepdims=True))
        probs = jnp.exp(scores - jnp.concatenate([top] * (rows // LANES), axis=1))
        acc[head] = acc[head] * jnp.exp(before - top) + dot_nn(probs.astype(BF), vals)
        peak[head] = top

    staged(range(GROUP), begin, finish)


def head_lanes(lane, head):
    at = stat_lane(head)
    return (lane >= at) & (lane < at + 3)


def own_kernel(tiles, rng, bias, fq, fk, weights, tok, lin, acc_out, peak_out, qa, peak, acc):
    rows = 2 * SLOT_TILE
    lax.fori_loop(0, tiles, projector(tok, lin, weights, bias), 0)
    lane = lanes_of(rows)

    def per_tile(tile, carry):
        make_queries(qa, lin, slot_start(tile), query_codes(fq, slot_start(tile + tiles)))
        for head in range(GROUP):
            peak[head] = jnp.full((rows, LANES), FLOOR_MAX, F32)
            acc[head] = jnp.zeros((rows, LANES), F32)

        def step(other, inner):
            code = both(fk, slot_start(other + tiles), slice(0, LANES))
            attend_step(qa, peak, acc, lin, slot_start(other), code)
            return inner

        low = jnp.maximum(rng[2 * tile] - tiles, 0)
        high = jnp.minimum(rng[2 * tile + 1] - tiles, tiles)
        lax.fori_loop(low, high, step, 0)
        peaks = jnp.zeros((rows, LANES), F32)
        for head in range(GROUP):
            acc_out[tile, head] = acc[head]
            peaks = jnp.where(head_lanes(lane, head), peak[head], peaks)
        peak_out[tile] = peaks
        return carry

    lax.fori_loop(0, tiles, per_tile, 0)


def far_kernel(
    tiles, rng, bias, fq, fk, weights, before, after, lin, acc_in, peak_in,
    ctx_out, ctx_r_out, stat_out, lin_before, lin_after, qa, peak, acc,
):
    rows = 2 * SLOT_TILE
    lane = lanes_of(rows)
    lax.fori_loop(
        jnp.minimum(rng[0], tiles), tiles, projector(before, lin_before, weights, bias), 0
    )
    lax.fori_loop(
        0,
        jnp.maximum(rng[2 * tiles - 1] - 2 * tiles, 0),
        projector(after, lin_after, weights, bias),
        0,
    )

    def per_tile(tile, carry):
        first = slot_start(tile)
        low, high = rng[2 * tile], rng[2 * tile + 1]
        end_before = jnp.minimum(high, tiles)
        start_after = jnp.maximum(low - 2 * tiles, 0)
        end_after = high - 2 * tiles
        for head in range(GROUP):
            acc[head] = acc_in[tile, head]
            at = stat_lane(head)
            peak[head] = jnp.broadcast_to(peak_in[tile][:, at : at + 1], (rows, LANES))

        @pl.when((low < end_before) | (start_after < end_after))
        def _():
            make_queries(qa, lin, first, query_codes(fq, slot_start(tile + tiles)))

            def step_before(other, inner):
                code = both(fk, slot_start(other), slice(0, LANES))
                attend_step(qa, peak, acc, lin_before, slot_start(other), code)
                return inner

            def step_after(other, inner):
                code = both(fk, slot_start(other + 2 * tiles), slice(0, LANES))
                attend_step(qa, peak, acc, lin_after, slot_start(other), code)
                return inner

            lax.fori_loop(low, end_before, step_before, 0)
            lax.fori_loop(start_after, end_after, step_after, 0)

        totals = jnp.ones((rows, LANES), F32)
        peaks = jnp.zeros((rows, LANES), F32)
        for head in range(GROUP):
            mine = head_lanes(lane, head)
            totals = jnp.where(mine, acc[head], totals)
            peaks = jnp.where(mine, peak[head], peaks)
        totals = jnp.maximum(totals, 1.0)
        level = -(peaks + jnp.log(totals))
        level = jnp.where(lane < HEAD_DIM, level, 0.0) + pltpu.roll(
            jnp.where(lane < HEAD_DIM, 0.0, level), HEAD_DIM, 1
        )
        high_part, mid_part, low_part = three_parts(level)
        turn = (lane - STAT_LANE) % 3
        stats = jnp.where(turn == 0, high_part, jnp.where(turn == 1, mid_part, low_part))
        stats = stats.astype(BF)
        inverse = 1.0 / totals
        for pair in range(PAIRED):
            left, right = (
                acc[head] * inverse[:, stat_lane(head) : stat_lane(head) + 1]
                for head in (2 * pair, 2 * pair + 1)
            )
            cells = jnp.where(lane < HEAD_DIM, left, right)
            cols = slice(pair * LANES, (pair + 1) * LANES)
            for seg in range(2):
                part = cells[seg * SLOT_TILE : (seg + 1) * SLOT_TILE]
                ctx_out[seg, pl.ds(first, SLOT_TILE), cols] = part
                ctx_r_out[seg, pl.ds(first, SLOT_TILE), cols] = part.astype(BF)
        for seg in range(2):
            stat_out[seg, pl.ds(first, SLOT_TILE), :] = stats[seg * SLOT_TILE : (seg + 1) * SLOT_TILE]
        return carry

    lax.fori_loop(0, tiles, per_tile, 0)


def delta_kernel(d_ctx, ctx, stat, pay_out):
    rows = d_ctx.shape[1]
    lane = lanes_of(rows)
    for seg in range(2):
        stats = stat[seg].astype(F32)
        for pair in range(PAIRED):
            cols = slice(pair * LANES, (pair + 1) * LANES)
            cells = d_ctx[seg, :, cols]
            pay_out[seg, :, cols] = cells
            product = cells.astype(F32) * ctx[seg, :, cols]
            for half in range(2):
                head = 2 * pair + half
                keep = lane < HEAD_DIM if half == 0 else lane >= HEAD_DIM
                delta = -jnp.sum(jnp.where(keep, product, 0.0), axis=1, keepdims=True)
                for k, part in enumerate(three_parts(delta)):
                    at = HEAD_DIM + STAT_LANE + 3 * head + k
                    stats = jnp.where(lane == at, part, stats)
        pay_out[seg, :, WIDE : WIDE + LANES] = stats.astype(BF)


def backward_kernel(tiles, rng, fq, fk, *rest):
    pays, lins = rest[:3], rest[3:6]
    dlin_out, lin, pay, qa, da, ka, va, acc_q, acc_k, acc_v, sems = rest[6:]
    rows = 2 * SLOT_TILE
    copy_all(block_copies(pays, pay, sems, 0) + block_copies(lins, lin, sems, 3))
    acc_k[...] = jnp.zeros_like(acc_k)
    acc_v[...] = jnp.zeros_like(acc_v)

    def keys_of(start, code, head):
        keys = both(lin, start, pair_cols(1, head))
        return jnp.where(in_head(head, rows), keys, code + ones_row(head, rows))

    def vals_of(start, head):
        vals = both(lin, start, pair_cols(2, head))
        return jnp.where(in_head(head, rows), vals, ones_row(head, rows))

    def queries_of(start):
        level, delta = spread_stats(both(pay, start, slice(WIDE, WIDE + LANES)))
        return query_codes(fq, start, level), delta

    def per_tile(tile, carry):
        here = slot_start(tile + tiles)
        codes, delta = queries_of(here)
        code_a = both(fk, here, slice(0, LANES))
        for head in range(GROUP):
            mine = in_head(head, rows)
            qa[head] = jnp.where(mine, both(lin, here, pair_cols(0, head)), codes)
            da[head] = jnp.where(mine, both(pay, here, pair_cols(0, head)), delta)
            ka[head] = keys_of(here, code_a, head)
            va[head] = vals_of(here, head)
            acc_q[head] = jnp.zeros((rows, LANES), F32)
        low, high = rng[2 * tile], rng[2 * tile + 1]

        def own_step(other, inner):
            start = slot_start(other)
            at = other - tiles
            code = both(fk, start, slice(0, LANES))

            def begin(head):
                keys = keys_of(start, code, head)
                return keys, dot_nt(qa[head], keys), dot_nt(da[head], vals_of(start, head))

            def finish(head, state):
                keys, scores, d_probs = state
                probs = jnp.exp(scores)
                d_scores = (probs * d_probs).astype(BF)
                acc_q[head] += dot_nn(d_scores, keys)
                acc_k[at, head] += dot_tn(d_scores, qa[head])
                acc_v[at, head] += dot_tn(probs.astype(BF), da[head])

            staged(range(GROUP), begin, finish)
            return inner

        lax.fori_loop(jnp.maximum(low, tiles), jnp.minimum(high, 2 * tiles), own_step, 0)
        before = jnp.maximum(jnp.minimum(high, tiles) - low, 0)
        upper = jnp.maximum(low, 2 * tiles)
        after = jnp.maximum(high - upper, 0)

        def far_step(index, inner):
            other = jnp.where(index < before, low + index, upper + index - before)
            start = slot_start(other)
            code = both(fk, start, slice(0, LANES))
            codes_b, delta_b = queries_of(start)

            def begin(item):
                head, side = item
                if side == 0:
                    keys = keys_of(start, code, head)
                    return keys, dot_nt(qa[head], keys), dot_nt(da[head], vals_of(start, head))
                mine = in_head(head, rows)
                query = jnp.where(mine, both(lin, start, pair_cols(0, head)), codes_b)
                d_ctx = jnp.where(mine, both(pay, start, pair_cols(0, head)), delta_b)
                return (query, d_ctx), dot_nt(ka[head], query), dot_nt(va[head], d_ctx)

            def finish(item, state):
                head, side = item
                operand, scores, d_probs = state
                probs = jnp.exp(scores)
                d_scores = (probs * d_probs).astype(BF)
                if side == 0:
                    acc_q[head] += dot_nn(d_scores, operand)
                else:
                    query, d_ctx = operand
                    acc_k[tile, head] += dot_nn(d_scores, query)
                    acc_v[tile, head] += dot_nn(probs.astype(BF), d_ctx)

            staged([(head, side) for head in range(GROUP) for side in range(2)], begin, finish)
            return inner

        lax.fori_loop(0, before + after, far_step, 0)
        put(acc_q, None, slot_start(tile), 0, 1.0 / math.sqrt(HEAD_DIM))
        return carry

    def put(acc, tile, first, part, scale):
        lower = lanes_of(rows) < HEAD_DIM
        for pair in range(PAIRED):
            sides = [2 * pair, 2 * pair + 1]
            left, right = (acc[k] if tile is None else acc[tile, k] for k in sides)
            cells = jnp.where(lower, left, right) * scale
            cells = cells.astype(BF)
            cols = slice(part * WIDE + pair * LANES, part * WIDE + (pair + 1) * LANES)
            for seg in range(2):
                dlin_out[seg, pl.ds(first, SLOT_TILE), cols] = cells[
                    seg * SLOT_TILE : (seg + 1) * SLOT_TILE
                ]

    lax.fori_loop(0, tiles, per_tile, 0)

    def last(tile, carry):
        put(acc_k, tile, slot_start(tile), 1, 1.0)
        put(acc_v, tile, slot_start(tile), 2, 1.0)
        return carry

    lax.fori_loop(0, tiles, last, 0)


def attend_scratch():
    rows = 2 * SLOT_TILE
    return [
        pltpu.VMEM((GROUP, rows, LANES), BF),
        pltpu.VMEM((GROUP, rows, LANES), F32),
        pltpu.VMEM((GROUP, rows, LANES), F32),
    ]


def attend_own(tok, weights, bias, fq, fk, rng):
    slots = tok.shape[1]
    tiles = slots // SLOT_TILE
    rows = 2 * SLOT_TILE
    shapes = [
        ((2, slots, 3 * WIDE), BF),
        ((tiles, GROUP, rows, LANES), F32),
        ((tiles, rows, LANES), F32),
    ]
    return pl.pallas_call(
        functools.partial(own_kernel, tiles),
        out_shape=tuple(jax.ShapeDtypeStruct(shape, kind) for shape, kind in shapes),
        grid=(1,),
        in_specs=[SMEM] + [whole(item.shape) for item in (bias, fq, fk, weights, tok)],
        out_specs=tuple(whole(shape) for shape, _ in shapes),
        scratch_shapes=attend_scratch(),
        compiler_params=vmem(20),
        cost_estimate=cost(1, 1),
        name="attend_own",
    )(rng, bias, fq, fk, weights, tok)


def attend_far(before, after, own, weights, bias, fq, fk, rng):
    slots = before.shape[1]
    tiles = slots // SLOT_TILE
    shapes = [
        ((2, slots, WIDE), F32),
        ((2, slots, WIDE), BF),
        ((2, slots, LANES), BF),
        ((2, slots, 3 * WIDE), BF),
        ((2, slots, 3 * WIDE), BF),
    ]
    return pl.pallas_call(
        functools.partial(far_kernel, tiles),
        out_shape=tuple(jax.ShapeDtypeStruct(shape, kind) for shape, kind in shapes),
        grid=(1,),
        in_specs=[SMEM]
        + [whole(item.shape) for item in (bias, fq, fk, weights, before, after, *own)],
        out_specs=tuple(whole(shape) for shape, _ in shapes),
        scratch_shapes=attend_scratch(),
        compiler_params=vmem(32),
        cost_estimate=cost(4, 8),
        name="attend_far",
    )(rng, bias, fq, fk, weights, before, after, *own)


def attend_back(lins, pays, fq, fk, rng):
    slots = pays[1].shape[1]
    tiles = slots // SLOT_TILE
    rows = 2 * SLOT_TILE
    return pl.pallas_call(
        functools.partial(backward_kernel, tiles),
        out_shape=jax.ShapeDtypeStruct((2, slots, 3 * WIDE), BF),
        grid=(1,),
        in_specs=[SMEM, whole(fq.shape), whole(fk.shape)] + [ANY] * 6,
        out_specs=whole((2, slots, 3 * WIDE)),
        scratch_shapes=[
            pltpu.VMEM((2, 3 * slots, 3 * WIDE), BF),
            pltpu.VMEM((2, 3 * slots, WIDE + LANES), BF),
            pltpu.VMEM((GROUP, rows, LANES), BF),
            pltpu.VMEM((GROUP, rows, LANES), BF),
            pltpu.VMEM((GROUP, rows, LANES), BF),
            pltpu.VMEM((GROUP, rows, LANES), BF),
            pltpu.VMEM((GROUP, rows, LANES), F32),
            pltpu.VMEM((tiles, GROUP, rows, LANES), F32),
            pltpu.VMEM((tiles, GROUP, rows, LANES), F32),
            pltpu.SemaphoreType.DMA((6,)),
        ],
        compiler_params=vmem(32),
        cost_estimate=cost(24, 12),
        name="attend_back",
    )(rng, fq, fk, *pays, *lins)


def payload(d_ctx, ctx, stat):
    slots = d_ctx.shape[1]
    return pl.pallas_call(
        delta_kernel,
        out_shape=jax.ShapeDtypeStruct((2, slots, WIDE + LANES), BF),
        grid=(1,),
        in_specs=[whole(d_ctx.shape), whole(ctx.shape), whole(stat.shape)],
        out_specs=whole((2, slots, WIDE + LANES)),
        compiler_params=vmem(10),
        cost_estimate=cost(0.5, 3),
        name="payload",
    )(d_ctx, ctx, stat)


def norm_forward(hidden):
    mean_val = jnp.mean(hidden, axis=-1, keepdims=True)
    centred = hidden - mean_val
    rate = lax.rsqrt(jnp.mean(centred * centred, axis=-1, keepdims=True) + EPS)
    return centred * rate, rate


def norm_backward(d_normal, normal, rate):
    return rate * (
        d_normal
        - jnp.mean(d_normal, axis=-1, keepdims=True)
        - normal * jnp.mean(d_normal * normal, axis=-1, keepdims=True)
    )


def normal_share(values):
    bell = jnp.exp(values * values * -0.5)
    t = 1.0 / (1.0 + (0.3275911 / math.sqrt(2.0)) * jnp.abs(values))
    poly = 0.5 * 1.061405429
    for term in (-1.453152027, 1.421413741, -0.284496736, 0.254829592):
        poly = poly * t + 0.5 * term
    beyond = poly * t * bell
    share = jnp.where(values < 0.0, beyond, 1.0 - beyond)
    return share, bell * (1.0 / math.sqrt(2.0 * math.pi))


def chain_kernel(
    tok, ctx_a, ctx_b, cot, wo_a, wo_b, vecs, up, up_bias, down,
    out, d_first_out, d_ctx_a, d_ctx_b, act_out, d_pre_out, normed_out, d_down_out, d_attn_out,
    sums, up_sums, slope,
):
    hidden = up.shape[1]
    chunk = min(512, hidden)

    @pl.when(pl.program_id(0) == 0)
    def _():
        sums[...] = jnp.zeros_like(sums)
        up_sums[...] = jnp.zeros_like(up_sums)

    out_bias, gain_1, shift_1, down_bias, gain_2, shift_2 = (vecs[k : k + 1, :] for k in range(6))

    def tally(row, cells):
        sums[row : row + 1, :] += jnp.sum(cells, axis=0, keepdims=True)

    first = (
        tok[0, 0].astype(F32)
        + (dot_nn(ctx_a[...], wo_a[...]) + dot_nn(ctx_b[...], wo_b[...]))
        + out_bias
    )
    normal_1, rate_1 = norm_forward(first)
    normed = normal_1 * gain_1 + shift_1
    normed_r = normed.astype(BF)
    normed_out[...] = normed_r
    second = [normed + down_bias]

    def columns(part):
        return slice(part * chunk, (part + 1) * chunk)

    def begin_up(part):
        return dot_nn(normed_r, up[:, columns(part)])

    def finish_up(part, lin):
        cols = columns(part)
        pre = lin + up_bias[:, cols]
        share, bell = normal_share(pre)
        slope[:, cols] = share + pre * bell
        act_r = (pre * share).astype(BF)
        act_out[:, cols] = act_r
        second[0] = second[0] + dot_nn(act_r, down[cols, :])

    staged(range(hidden // chunk), begin_up, finish_up, 1)
    second = second[0]
    normal_2, rate_2 = norm_forward(second)
    out[...] = (normal_2 * gain_2 + shift_2).astype(BF)
    d_out = cot[0, 0].astype(F32)
    tally(4, d_out * normal_2)
    tally(5, d_out)
    d_second = norm_backward(d_out * gain_2, normal_2, rate_2)
    tally(3, d_second)
    d_down_r = d_second.astype(BF)
    d_down_out[...] = d_down_r
    d_normed = [d_second]

    def begin_down(part):
        return dot_nt(d_down_r, down[columns(part), :])

    def finish_down(part, d_act):
        cols = columns(part)
        d_pre_r = (d_act * slope[:, cols]).astype(BF)
        d_pre_out[:, cols] = d_pre_r
        up_sums[0:1, cols] += jnp.sum(d_pre_r.astype(F32), axis=0, keepdims=True)
        d_normed[0] = d_normed[0] + dot_nt(d_pre_r, up[:, cols])

    staged(range(hidden // chunk), begin_down, finish_down, 1)
    d_normed = d_normed[0]
    tally(1, d_normed * normal_1)
    tally(2, d_normed)
    d_first = norm_backward(d_normed * gain_1, normal_1, rate_1)
    tally(0, d_first)
    d_first_out[...] = d_first
    d_attn_r = d_first.astype(BF)
    d_attn_out[...] = d_attn_r
    d_ctx_a[...] = dot_nt(d_attn_r, wo_a[...]).astype(BF)
    d_ctx_b[...] = dot_nt(d_attn_r, wo_b[...]).astype(BF)


def chain(micro, tokens, ctx_a, ctx_b, cotangent, wo_a, wo_b, vecs, up, up_bias, down):
    slots, model = tokens.shape[2:]
    hidden = up.shape[1]
    rows = min(CHAIN_ROWS, slots)
    of_micro = pl.BlockSpec((1, 1, rows, model), lambda i: (micro, 0, i, 0))
    sizes = [
        (model, BF), (model, F32), (WIDE, BF), (WIDE, BF), (hidden, BF), (hidden, BF),
        (model, BF), (model, BF), (model, BF),
    ]
    return pl.pallas_call(
        chain_kernel,
        out_shape=tuple(jax.ShapeDtypeStruct((slots, cols), kind) for cols, kind in sizes)
        + (jax.ShapeDtypeStruct((8, model), F32), jax.ShapeDtypeStruct((8, hidden), F32)),
        grid=(slots // rows,),
        in_specs=[
            of_micro,
            row_block(rows, WIDE),
            row_block(rows, WIDE),
            of_micro,
            whole(wo_a.shape),
            whole(wo_b.shape),
            whole(vecs.shape),
            whole(up.shape),
            whole(up_bias.shape),
            whole(down.shape),
        ],
        out_specs=tuple(row_block(rows, cols) for cols, _ in sizes)
        + (whole((8, model)), whole((8, hidden))),
        scratch_shapes=[pltpu.VMEM((rows, hidden), F32)],
        compiler_params=vmem(28),
        cost_estimate=cost(6, 12),
        name="chain",
    )(tokens, ctx_a, ctx_b, cotangent, wo_a, wo_b, vecs, up, up_bias, down)


def weight_kernel(*refs):
    acts, d_downs, normeds, d_pres, d_attns, ctx_as, ctx_bs, sums, up_sums = (
        refs[2 * k : 2 * k + 2] for k in range(9)
    )
    seg, out = refs[18], refs[19]
    step = pl.program_id(0)
    width = out.shape[1]
    parts = up_sums[0].shape[1] // width

    def summed(lefts, rights):
        left = jnp.concatenate([item[...] for item in lefts], axis=0)
        return dot_tn(left, jnp.concatenate([item[...] for item in rights], axis=0)).astype(BF)

    @pl.when(step < parts)
    def _():
        out[...] = summed(acts, d_downs)

    @pl.when((step >= parts) & (step < 2 * parts))
    def _():
        out[...] = summed(normeds, d_pres)

    @pl.when((step == 2 * parts) & (seg[0] == 0))
    def _():
        out[:WIDE, :] = summed(ctx_as, d_attns)
        out[WIDE:, :] = summed(ctx_bs, d_attns)

    @pl.when((step == 2 * parts) & (seg[0] != 0))
    def _():
        out[:WIDE, :] = summed(ctx_bs, d_attns)
        out[WIDE:, :] = summed(ctx_as, d_attns)

    @pl.when(step == 2 * parts + 1)
    def _():
        wide = up_sums[0][0:1, :] + up_sums[1][0:1, :]
        cells = [sums[0][...] + sums[1][...]]
        cells += [wide[:, k * width : (k + 1) * width] for k in range(parts)]
        cells += [jnp.zeros((width - 8 - parts, width), F32)]
        out[...] = jnp.concatenate(cells, axis=0).astype(BF)


def weight_grads(groups, seg, model):
    flat = [item for group in groups for item in group]
    slots, hidden = groups[0][0].shape
    parts = hidden // model

    def fixed(item):
        return pl.BlockSpec(item.shape, lambda i: (0, 0))

    def column(first):
        return pl.BlockSpec((slots, model), lambda i: (0, jnp.clip(i - first, 0, parts - 1)))

    specs = [column(0)] * 2
    specs += [fixed(item) for item in groups[1] + groups[2]]
    specs += [column(parts)] * 2
    specs += [fixed(item) for group in groups[4:] for item in group]
    return pl.pallas_call(
        weight_kernel,
        out_shape=pltpu.HBM(((2 * parts + 1) * model + 16, model), BF),
        grid=(2 * parts + 2,),
        in_specs=specs + [SMEM],
        out_specs=row_block(model, model),
        compiler_params=vmem(24),
        cost_estimate=cost(1, 2),
        name="weight_grads",
    )(*flat, seg)


def unpack_kernel(parts, cells, down_out, up_out, out_out):
    step = pl.program_id(0)

    @pl.when(step < parts)
    def _():
        down_out[...] = cells[...].astype(F32)

    @pl.when((step >= parts) & (step < 2 * parts))
    def _():
        up_out[...] = cells[...].astype(F32)

    @pl.when(step == 2 * parts)
    def _():
        out_out[...] = cells[...].astype(F32)


def unpack(cells, hidden):
    model = cells.shape[1]
    parts = hidden // model
    block = (model, model)
    return pl.pallas_call(
        functools.partial(unpack_kernel, parts),
        out_shape=(
            jax.ShapeDtypeStruct((hidden, model), F32),
            jax.ShapeDtypeStruct((model, hidden), F32),
            jax.ShapeDtypeStruct((model, model), F32),
        ),
        grid=(2 * parts + 1,),
        in_specs=[pl.BlockSpec(block, lambda i: (i, 0))],
        out_specs=(
            pl.BlockSpec(block, lambda i: (jnp.minimum(i, parts - 1), 0)),
            pl.BlockSpec(block, lambda i: (0, jnp.clip(i - parts, 0, parts - 1))),
            pl.BlockSpec(block, lambda i: (0, 0)),
        ),
        compiler_params=vmem(12),
        cost_estimate=cost(0.1, 16),
        name="unpack",
    )(cells)


def qkv_weight_kernel(micros, *refs):
    joints, d_lins, out = refs[:micros], refs[micros : 2 * micros], refs[-1]
    slots, model = joints[0].shape[1:]
    total = jnp.zeros((model, WIDE), F32)
    sums = jnp.zeros((1, WIDE), F32)
    for m in range(micros):
        for seg in range(2):
            cells = d_lins[m][seg]
            total = total + dot_tn(joints[m][seg], cells)
            sums = sums + jnp.sum(cells.astype(F32), axis=0, keepdims=True)
    out[:model, :] = total.astype(BF)
    first = lax.broadcasted_iota(jnp.int32, (16, WIDE), 0) == 0
    out[model : model + 16, :] = jnp.where(first, sums, 0.0).astype(BF)
    if out.shape[0] > model + 16:
        out[model + 16 :, :] = jnp.zeros((out.shape[0] - model - 16, WIDE), BF)


def qkv_weight_grad(joints, d_lins, after, rows):
    slots, model = joints[0].shape[1:]
    return pl.pallas_call(
        functools.partial(qkv_weight_kernel, len(joints)),
        out_shape=jax.ShapeDtypeStruct((rows, 3 * WIDE), BF),
        grid=(3,),
        in_specs=[pl.BlockSpec((2, slots, model), lambda i: (0, 0, 0))] * len(joints)
        + [pl.BlockSpec((2, slots, WIDE), lambda i: (0, 0, i))] * len(joints)
        + [ANY],
        out_specs=pl.BlockSpec((rows, WIDE), lambda i: (0, i)),
        compiler_params=vmem(20),
        cost_estimate=cost(1.6, 4),
        name="qkv_weight_grad",
    )(*joints, *d_lins, after)


def finish_kernel(cells, *refs):
    micros = (len(refs) - 3) // 2
    near, far = refs[:micros], refs[micros : 2 * micros]
    out, small, token_out = refs[2 * micros :]
    rows = out.shape[0]
    for seg in range(2):
        for part in range(3):
            first = (2 * part + seg) * WIDE
            block = cells[seg, :rows, part * WIDE : (part + 1) * WIDE]
            out[:, first : first + WIDE] = block.astype(F32)
    edge = cells[:, rows : rows + 16, :].astype(F32)
    small[...] = jnp.concatenate(
        [edge[seg, :, part * WIDE : (part + 1) * WIDE] for part in (0, 2) for seg in range(2)],
        axis=1,
    )
    for m in range(micros):
        token_out[m, 0] = near[m][...] + far[m][...].astype(F32)


def finish(cells, near, far):
    slots, model = near[0].shape
    shapes = [
        ((model, 6 * WIDE), F32),
        ((16, 4 * WIDE), F32),
        ((len(near), 1, slots, model), F32),
    ]
    flat = [cells, *near, *far]
    return pl.pallas_call(
        finish_kernel,
        out_shape=tuple(jax.ShapeDtypeStruct(shape, kind) for shape, kind in shapes),
        grid=(1,),
        in_specs=[whole(item.shape) for item in flat],
        out_specs=tuple(whole(shape) for shape, _ in shapes),
        compiler_params=vmem(28),
        cost_estimate=cost(0.1, 12),
        name="finish",
    )(*flat)


def swapped(value):
    return lax.ppermute(value, "seg", [(0, 1), (1, 0)])


def shifted(value, by):
    size = lax.axis_size("seq")
    return lax.ppermute(
        value, "seq", [(i, i + by) for i in range(size) if 0 <= i + by < size]
    )


def flipped(value, bit):
    return lax.ppermute(value, "seq", [(i, i ^ bit) for i in range(lax.axis_size("seq"))])


def pick(value, index, axis):
    zero = jnp.int32(0)
    starts = [zero] * value.ndim
    starts[axis] = lax.convert_element_type(index, jnp.int32)
    sizes = list(value.shape)
    sizes[axis] = 1
    part = lax.dynamic_slice(value, starts, sizes)
    return lax.reshape(part, value.shape[:axis] + value.shape[axis + 1 :])


def stacked(pieces):
    return lax.concatenate([lax.expand_dims(piece, (0,)) for piece in pieces], 0)


def by_segment(mine, other, seg):
    return lax.select(seg == 0, stacked([mine, other]), stacked([other, mine]))


def bit_groups(size):
    bits = size.bit_length() - 1
    groups = [(k, 1) for k in range(min(bits, 2))]
    groups += [(k, min(2, bits - k)) for k in range(2, bits, 2)]
    return groups


def moved(value, seg_flip, seq_flip):
    size = lax.axis_size("seq")
    total = size * lax.axis_size("seg")
    pairs = [(i, i ^ (seg_flip * size + seq_flip)) for i in range(total)]
    return lax.ppermute(value, ("seg", "seq"), pairs)


def scatter_seq(cells, seq):
    for shift, count in bit_groups(lax.axis_size("seq")):
        own = lax.bitwise_and(lax.shift_right_logical(seq, jnp.int32(shift)), jnp.int32(2**count - 1))
        split = cells.reshape((-1, 2**count) + cells.shape[1:])
        total = pick(split, own, 1).astype(F32)
        for turn in range(1, 2**count):
            total = total + moved(pick(split, own ^ turn, 1), 0, turn << shift).astype(F32)
        cells = total.astype(BF)
    return cells


def merged(cells, first, second):
    order = [k for k in range(cells.ndim) if k != first]
    order.insert(second, first)
    shape = [cells.shape[k] for k in order]
    if cells.shape[order[second - 1]] > 1:
        cells = lax.transpose(cells, order)
    shape[second - 1 : second + 1] = [shape[second - 1] * shape[second]]
    return lax.reshape(cells, shape)


def in_order(pieces, own):
    bit = 1
    pieces = list(pieces)
    while bit < len(pieces):
        turned = lax.ne(lax.bitwise_and(own, jnp.int32(bit)), jnp.int32(0))
        pieces = [
            lax.select(turned, pieces[k ^ bit], pieces[k]) for k in range(len(pieces))
        ]
        bit *= 2
    return stacked(pieces)


def gather_all(cells, seg, seq):
    groups = bit_groups(lax.axis_size("seq"))[::-1]
    for at, (shift, count) in enumerate(groups):
        turns = [turn << shift for turn in range(2**count)]
        own = lax.bitwise_and(lax.shift_right_logical(seq, jnp.int32(shift)), jnp.int32(2**count - 1))
        if at == max(len(groups) - 2, 0):
            sides = [
                in_order([moved(cells, g, t) if g or t else cells for t in turns], own)
                for g in range(2)
            ]
            cells = merged(in_order(sides, seg), 1, 2)
        else:
            pieces = in_order([moved(cells, 0, t) if t else cells for t in turns], own)
            cells = merged(pieces, 0, cells.ndim - 2)
    return cells


def code_tables(lengths, base, slots, extent):
    spans = jnp.maximum(lengths[:, 0], lengths[:, 1])
    count = spans.shape[1]
    order = jnp.arange(count, dtype=jnp.int32)
    ends = jnp.sum(jnp.where(order[None, :] <= order[:, None], spans[:, None, :], 0), axis=2)
    place = base + jnp.arange(extent, dtype=jnp.int32)
    past = ends[:, None, :] <= place[None, :, None]
    pair = jnp.sum(past.astype(jnp.int32), axis=2)
    start = jnp.sum(jnp.where(past, spans[:, None, :], 0), axis=2)
    here = order[None, None, :] == pair[:, :, None]
    stop = jnp.sum(jnp.where(here, ends[:, None, :], 0), axis=2)
    inside = (pair < count) & (place >= 0)[None, :]
    counts = [jnp.sum(jnp.where(here, lengths[:, c, None, :], 0), axis=2) for c in range(2)]
    valid = jnp.stack(
        [inside & (place[None, :] - start < counts[c]) for c in range(2)], axis=1
    )
    lane = jnp.arange(LANES, dtype=jnp.int32) % HEAD_DIM
    digits = [pair, pair // DIGIT, pair // (DIGIT * DIGIT)]
    hot = jnp.zeros(pair.shape + (LANES,), bool)
    for k, digit in enumerate(digits):
        hot = hot | (lane == (digit % DIGIT)[:, :, None] + k * DIGIT)
    hot = hot & inside[:, :, None]
    is_code = lane <= BAD_LANE
    fq = jnp.where(is_code & ~hot, MASK_OFF, 0.0).astype(BF)
    bad = (lane == BAD_LANE) & ~valid[:, :, :, None]
    fk = (hot[:, None] | bad).astype(BF)
    low = jnp.where(inside, start, place[None, :])
    high = jnp.where(inside, stop, place[None, :])
    first = extent // 3
    low = jnp.clip(low[:, first : first + slots : SLOT_TILE] - base, 0, extent)
    last = first + SLOT_TILE - 1
    high = jnp.clip(high[:, last : first + slots : SLOT_TILE] - base, 0, extent)
    rng = jnp.stack([low // SLOT_TILE, -(-high // SLOT_TILE)], axis=2)
    return fq, fk, rng.reshape(rng.shape[0], -1).astype(jnp.int32)


def second_half(seg, seq, pays, forwards, owns, fq, fk, rng, joint, own_cols, d_firsts):
    micros = len(pays)
    ring = lax.axis_size("seq")
    slots, model = joint[0].shape[1:]
    d_lins, near, far = [], [], []
    pays = [*pays[:-1], (shifted(pays[-1], 1), pays[-1], shifted(pays[-1], -1))]
    for m in range(micros):
        lins = (forwards[m][3], owns[m][0], forwards[m][4])
        d_lin = attend_back(lins, pays[m], fq[m], fk[m], rng[m])
        d_lins.append(d_lin)
        far.append(swapped(dot_nt(pick(d_lin, 1 - seg, 0), own_cols).astype(BF)))
        near.append(d_firsts[m] + dot_nt(pick(d_lin, seg, 0), own_cols))
    late = model + 8 * max(ring, 16)
    qkv = qkv_weight_grad(joint, d_lins, far[0], late).reshape(ring, late // ring, 3 * WIDE)
    qkv = scatter_seq(qkv, seq)
    qkv, far[-1], near[-1] = lax.optimization_barrier((qkv, far[-1], near[-1]))
    qkv = gather_all(qkv, seg, seq).reshape(2, late, 3 * WIDE)
    qkv_grad, late_sums, token_grads = finish(qkv, near, far)
    return token_grads, qkv_grad, late_sums


def per_device(
    tokens,
    lengths,
    qkv_weight,
    query_bias,
    value_bias,
    out_weight,
    out_bias,
    attn_gain,
    attn_shift,
    up_weight,
    up_bias,
    down_weight,
    down_bias,
    ffn_gain,
    ffn_shift,
    cotangent,
):
    seg = lax.axis_index("seg")
    seq = lax.axis_index("seq")
    ring = lax.axis_size("seq")
    micros, _, slots, model = tokens.shape
    hidden = up_weight.shape[1]
    extent = 3 * slots
    mine = [tokens[m, 0] for m in range(micros)]
    joint = []
    partner = None
    for m in range(micros):
        sent = mine[m]
        if m:
            sent, partner = lax.optimization_barrier((sent, partner))
            joint[-1] = by_segment(mine[m - 1], partner, seg)
        partner = swapped(sent)
        joint.append(by_segment(sent, partner, seg))
    before, after = [], []
    fq, fk, rng = code_tables(lengths, seq * slots - slots, slots, extent)
    own_cols = pick(qkv_weight.reshape(model, 3, 2, WIDE), seg, 2).reshape(model, 3 * WIDE)
    own_bias = jnp.concatenate(
        [
            pick(query_bias.reshape(2, WIDE), seg, 0),
            jnp.zeros((WIDE,), query_bias.dtype),
            pick(value_bias.reshape(2, WIDE), seg, 0),
        ]
    ).astype(F32)
    own_bias = jnp.broadcast_to(own_bias, (8, 3 * WIDE))
    halves = out_weight.reshape(2, WIDE, model)
    wo_a, wo_b = pick(halves, seg, 0), pick(halves, 1 - seg, 0)
    vecs = jnp.stack(
        [out_bias, attn_gain, attn_shift, down_bias, ffn_gain, ffn_shift, out_bias, out_bias]
    ).astype(F32)
    up_row = up_bias.astype(F32)[None, :]
    before.append(shifted(joint[0], 1))
    after.append(shifted(joint[0], -1))
    owns = [attend_own(joint[m], own_cols, own_bias, fq[m], fk[m], rng[m]) for m in range(micros)]
    for m in range(1, micros):
        sent, before[-1], after[-1], owns = lax.optimization_barrier(
            (joint[m], before[-1], after[-1], owns)
        )
        before.append(shifted(sent, 1))
        after.append(shifted(sent, -1))
    forwards = [
        attend_far(before[m], after[m], owns[m], own_cols, own_bias, fq[m], fk[m], rng[m])
        for m in range(micros)
    ]
    chains, contexts = [], []
    for m in range(micros):
        ctx_r = forwards[m][1]
        contexts.append((pick(ctx_r, seg, 0), swapped(pick(ctx_r, 1 - seg, 0))))
    contexts[0], forwards = lax.optimization_barrier((contexts[0], forwards))
    for m in range(micros):
        chains.append(
            chain(
                m, tokens, *contexts[m], cotangent, wo_a, wo_b, vecs, up_weight, up_row, down_weight
            )
        )
    def paid(m, arrived):
        return payload(by_segment(chains[m][2], arrived, seg), forwards[m][0], forwards[m][2])

    arrived = [swapped(item[3]) for item in chains]
    pays = [paid(m, arrived[m]) for m in range(micros - 1)]
    columns = [[item[k] for item in chains] for k in range(len(chains[0]))]
    columns[4], pays = lax.optimization_barrier((columns[4], pays))
    grads = weight_grads(
        [columns[4], columns[7], columns[6], columns[5], columns[8]]
        + [[c[0] for c in contexts], [c[1] for c in contexts]]
        + [columns[9], columns[10]],
        jnp.reshape(seg, (1,)).astype(jnp.int32),
        model,
    )
    pays = [(shifted(pay, 1), pay, shifted(pay, -1)) for pay in pays]
    grads, late, pays = lax.optimization_barrier((grads, arrived[-1], pays))
    grads = lax.psum(grads, ("seg", "seq"))
    pays.append(paid(micros - 1, late))
    d_firsts = [item[1] for item in chains]
    given = (pays, forwards, owns, fq, fk, rng, joint, own_cols, d_firsts)

    def taken(given):
        return second_half(seg, seq, *given)

    def empty(given):
        shapes = jax.eval_shape(taken, given)
        return jax.tree.map(lambda item: jnp.zeros(item.shape, item.dtype), shapes)

    token_grads, qkv_grad, late_sums = lax.cond(lengths[0, 0, 0] >= 0, taken, empty, given)
    down_grad, up_grad, out_grad = unpack(grads, hidden)
    tail = grads[2 * hidden + model : 2 * hidden + model + 16].astype(F32)
    return (
        jnp.stack([item[0] for item in chains])[:, None],
        token_grads,
        qkv_grad,
        late_sums[0, :model],
        late_sums[0, model:],
        out_grad,
        tail[0],
        tail[1],
        tail[2],
        up_grad,
        tail[8 : 8 + hidden // model].reshape(-1),
        down_grad,
        tail[3],
        tail[4],
        tail[5],
    )


def solution(mesh):
    split = P(None, "seg", "seq", None)
    return jax.shard_map(
        per_device,
        mesh=mesh,
        in_specs=(split,) + (P(),) * 14 + (split,),
        out_specs=(split, split) + (P(),) * 13,
        check_vma=False,
    )
```

```python
import functools
import math

import jax
import jax.numpy as jnp
from jax import lax
from jax.experimental import pallas as pl
from jax.experimental.pallas import tpu as pltpu
from jax.sharding import PartitionSpec as P

HEADS = 8
HEAD_DIM = 64
LONGEST = 512
FLOOR_MAX = -10000.0
MASK_OFF = -1e30
EPS = 1e-12
LANES = 128
SLOT_TILE = 128
DIGIT = 13
DIGITS = 3
BAD_LANE = DIGIT * DIGITS
STAT_LANE = BAD_LANE + 1
GROUP = HEADS // 2
WIDE = GROUP * HEAD_DIM
PAIRED = WIDE // LANES
CHAIN_ROWS = 256
BF = jnp.bfloat16
F32 = jnp.float32
ANY = pl.BlockSpec(memory_space=pl.ANY)
SMEM = pl.BlockSpec(memory_space=pltpu.SMEM)


def whole(shape):
    zeros = (0,) * len(shape)
    return pl.BlockSpec(shape, lambda _: zeros)


def row_block(rows, cols):
    return pl.BlockSpec((rows, cols), lambda i: (i, 0))


def vmem(mega):
    return pltpu.CompilerParams(vmem_limit_bytes=mega * 1024 * 1024)


def cost(giga, mega):
    return pl.CostEstimate(
        flops=int(giga * 10**9), bytes_accessed=int(mega * 10**6), transcendentals=0
    )


def dot_nn(left, right):
    return lax.dot_general(left, right, (((1,), (0,)), ((), ())), preferred_element_type=F32)


def dot_nt(left, right):
    return lax.dot_general(left, right, (((1,), (1,)), ((), ())), preferred_element_type=F32)


def dot_tn(left, right):
    return lax.dot_general(left, right, (((0,), (0,)), ((), ())), preferred_element_type=F32)


def lanes_of(rows):
    return lax.broadcasted_iota(jnp.int32, (rows, LANES), 1)


def in_head(head, rows):
    lane = lanes_of(rows)
    return lane < HEAD_DIM if head % 2 == 0 else lane >= HEAD_DIM


def stat_lane(head):
    return STAT_LANE + 3 * head + (HEAD_DIM if head % 2 == 0 else 0)


def ones_row(head, rows):
    lane = lanes_of(rows)
    first = stat_lane(head)
    return ((lane >= first) & (lane < first + 3)).astype(F32).astype(BF)


def pair_cols(part, head):
    first = part * WIDE + (head // 2) * LANES
    return slice(first, first + LANES)


def both(ref, start, cols):
    return jnp.concatenate(
        [ref[seg, pl.ds(start, SLOT_TILE), cols] for seg in range(2)], axis=0
    )


def three_parts(values):
    high = values.astype(BF).astype(F32)
    rest = values - high
    mid = rest.astype(BF).astype(F32)
    low = (rest - mid).astype(BF).astype(F32)
    return high, mid, low


def copy_all(copies):
    for item in copies:
        item.start()
    for item in copies:
        item.wait()


def block_copies(blocks, scratch, sems, first):
    rows = scratch.shape[1] // 3
    return [
        pltpu.make_async_copy(
            block, scratch.at[:, pl.ds(at * rows, rows), :], sems.at[first + at]
        )
        for at, block in enumerate(blocks)
    ]


def slot_start(tile):
    return pl.multiple_of(tile * SLOT_TILE, SLOT_TILE)


def query_codes(fq, start, level=None):
    codes = fq[pl.ds(start, SLOT_TILE), :]
    codes = jnp.concatenate([codes, codes], axis=0)
    return codes if level is None else codes + level


def spread_stats(stats):
    wide = stats.astype(F32)
    rolled = pltpu.roll(wide, HEAD_DIM, 1)
    lower = lanes_of(stats.shape[0]) < HEAD_DIM
    level = jnp.where(lower, wide, rolled)
    delta = jnp.where(lower, rolled, wide)
    return level.astype(BF), delta.astype(BF)


def staged(items, begin, finish, ahead=2):
    held = []
    for item in items:
        held.append((item, begin(item)))
        if len(held) > ahead:
            finish(*held.pop(0))
    for entry in held:
        finish(*entry)


def projector(tok, lin, weights, bias):
    rows = 2 * SLOT_TILE

    def project(tile, carry):
        start = slot_start(tile)
        cells = dot_nn(both(tok, start, slice(0, tok.shape[2])), weights[...])
        cells = (cells + bias[0:1, :]).astype(BF)
        for part in range(3):
            cols = slice(part * WIDE, (part + 1) * WIDE)
            piece = cells[:, cols]
            if part == 0:
                piece = piece * (1.0 / math.sqrt(HEAD_DIM))
            for seg in range(2):
                lin[seg, pl.ds(start, SLOT_TILE), cols] = piece[
                    seg * SLOT_TILE : (seg + 1) * SLOT_TILE
                ]
        return carry

    return project


def make_queries(qa, lin, start, codes):
    rows = 2 * SLOT_TILE
    for head in range(GROUP):
        qa[head] = jnp.where(in_head(head, rows), both(lin, start, pair_cols(0, head)), codes)


def attend_step(qa, peak, acc, lin, start, code):
    rows = 2 * SLOT_TILE

    def begin(head):
        keys = both(lin, start, pair_cols(1, head))
        keys = jnp.where(in_head(head, rows), keys, code)
        return dot_nt(qa[head], keys)

    def finish(head, scores):
        vals = both(lin, start, pair_cols(2, head))
        vals = jnp.where(in_head(head, rows), vals, ones_row(head, rows))
        before = peak[head]
        top = jnp.maximum(before, jnp.max(scores, axis=1, keepdims=True))
        probs = jnp.exp(scores - jnp.concatenate([top] * (rows // LANES), axis=1))
        acc[head] = acc[head] * jnp.exp(before - top) + dot_nn(probs.astype(BF), vals)
        peak[head] = top

    staged(range(GROUP), begin, finish)


def head_lanes(lane, head):
    at = stat_lane(head)
    return (lane >= at) & (lane < at + 3)


def own_kernel(tiles, rng, bias, fq, fk, weights, tok, lin, acc_out, peak_out, qa, peak, acc):
    rows = 2 * SLOT_TILE
    lax.fori_loop(0, tiles, projector(tok, lin, weights, bias), 0)
    lane = lanes_of(rows)

    def per_tile(tile, carry):
        make_queries(qa, lin, slot_start(tile), query_codes(fq, slot_start(tile)))
        for head in range(GROUP):
            peak[head] = jnp.full((rows, LANES), FLOOR_MAX, F32)
            acc[head] = jnp.zeros((rows, LANES), F32)

        def step(other, inner):
            code = both(fk, slot_start(other), slice(0, LANES))
            attend_step(qa, peak, acc, lin, slot_start(other), code)
            return inner

        low = jnp.maximum(rng[2 * tile] - tiles, 0)
        high = jnp.minimum(rng[2 * tile + 1] - tiles, tiles)
        lax.fori_loop(low, high, step, 0)
        peaks = jnp.zeros((rows, LANES), F32)
        for head in range(GROUP):
            acc_out[tile, head] = acc[head]
            peaks = jnp.where(head_lanes(lane, head), peak[head], peaks)
        peak_out[tile] = peaks
        return carry

    lax.fori_loop(0, tiles, per_tile, 0)


def far_kernel(
    tiles, rng, bias, fq, fk_before, fk_after, weights, before, after, lin, acc_in, peak_in,
    ctx_out, ctx_r_out, stat_out, before_out, after_out, qa, peak, acc, lin_before, lin_after, sems,
):
    rows = 2 * SLOT_TILE
    lane = lanes_of(rows)
    reach = (
        (before, lin_before, before_out, jnp.minimum(rng[0], tiles), tiles, 0),
        (after, lin_after, after_out, 0, jnp.maximum(rng[2 * tiles - 1] - 2 * tiles, 0), tiles),
    )

    def kept(side, tile):
        _, scratch, out, _, _, base = side
        some = pl.ds(slot_start(tile), SLOT_TILE)
        return pltpu.make_async_copy(
            scratch.at[:, some, :], out.at[:, some, :], sems.at[base + tile]
        )

    for side in reach:
        project = projector(side[0], side[1], weights, bias)

        def fill(tile, carry, side=side, project=project):
            project(tile, carry)
            kept(side, tile).start()
            return carry

        lax.fori_loop(side[3], side[4], fill, 0)

    def per_tile(tile, carry):
        first = slot_start(tile)
        low, high = rng[2 * tile], rng[2 * tile + 1]
        end_before = jnp.minimum(high, tiles)
        start_after = jnp.maximum(low - 2 * tiles, 0)
        end_after = high - 2 * tiles
        for head in range(GROUP):
            acc[head] = acc_in[tile, head]
            at = stat_lane(head)
            peak[head] = jnp.broadcast_to(peak_in[tile][:, at : at + 1], (rows, LANES))

        @pl.when((low < end_before) | (start_after < end_after))
        def _():
            make_queries(qa, lin, first, query_codes(fq, first))

            def step_before(other, inner):
                code = both(fk_before, slot_start(other), slice(0, LANES))
                attend_step(qa, peak, acc, lin_before, slot_start(other), code)
                return inner

            def step_after(other, inner):
                code = both(fk_after, slot_start(other), slice(0, LANES))
                attend_step(qa, peak, acc, lin_after, slot_start(other), code)
                return inner

            lax.fori_loop(low, end_before, step_before, 0)
            lax.fori_loop(start_after, end_after, step_after, 0)

        totals = jnp.ones((rows, LANES), F32)
        peaks = jnp.zeros((rows, LANES), F32)
        for head in range(GROUP):
            mine = head_lanes(lane, head)
            totals = jnp.where(mine, acc[head], totals)
            peaks = jnp.where(mine, peak[head], peaks)
        totals = jnp.maximum(totals, 1.0)
        level = -(peaks + jnp.log(totals))
        level = jnp.where(lane < HEAD_DIM, level, 0.0) + pltpu.roll(
            jnp.where(lane < HEAD_DIM, 0.0, level), HEAD_DIM, 1
        )
        high_part, mid_part, low_part = three_parts(level)
        turn = (lane - STAT_LANE) % 3
        stats = jnp.where(turn == 0, high_part, jnp.where(turn == 1, mid_part, low_part))
        stats = stats.astype(BF)
        inverse = 1.0 / totals
        for pair in range(PAIRED):
            left, right = (
                acc[head] * inverse[:, stat_lane(head) : stat_lane(head) + 1]
                for head in (2 * pair, 2 * pair + 1)
            )
            cells = jnp.where(lane < HEAD_DIM, left, right)
            cols = slice(pair * LANES, (pair + 1) * LANES)
            for seg in range(2):
                part = cells[seg * SLOT_TILE : (seg + 1) * SLOT_TILE]
                ctx_out[seg, pl.ds(first, SLOT_TILE), cols] = part
                ctx_r_out[seg, pl.ds(first, SLOT_TILE), cols] = part.astype(BF)
        for seg in range(2):
            stat_out[seg, pl.ds(first, SLOT_TILE), :] = stats[seg * SLOT_TILE : (seg + 1) * SLOT_TILE]
        return carry

    lax.fori_loop(0, tiles, per_tile, 0)
    for side in reach:

        def settle(tile, carry, side=side):
            kept(side, tile).wait()
            return carry

        lax.fori_loop(side[3], side[4], settle, 0)


def delta_kernel(d_ctx, ctx, stat, pay_out):
    rows = d_ctx.shape[1]
    lane = lanes_of(rows)
    for seg in range(2):
        stats = stat[seg].astype(F32)
        for pair in range(PAIRED):
            cols = slice(pair * LANES, (pair + 1) * LANES)
            cells = d_ctx[seg, :, cols]
            pay_out[seg, :, cols] = cells
            product = cells.astype(F32) * ctx[seg, :, cols]
            for half in range(2):
                head = 2 * pair + half
                keep = lane < HEAD_DIM if half == 0 else lane >= HEAD_DIM
                delta = -jnp.sum(jnp.where(keep, product, 0.0), axis=1, keepdims=True)
                for k, part in enumerate(three_parts(delta)):
                    at = HEAD_DIM + STAT_LANE + 3 * head + k
                    stats = jnp.where(lane == at, part, stats)
        pay_out[seg, :, WIDE : WIDE + LANES] = stats.astype(BF)


def backward_kernel(tiles, rng, fq, fk, *rest):
    pays, lins = rest[:3], rest[3:6]
    dlin_out, lin, pay, qa, da, ka, va, acc_q, acc_k, acc_v, sems = rest[6:]
    rows = 2 * SLOT_TILE
    copy_all(block_copies(pays, pay, sems, 0) + block_copies(lins, lin, sems, 3))
    acc_k[...] = jnp.zeros_like(acc_k)
    acc_v[...] = jnp.zeros_like(acc_v)

    def keys_of(start, code, head):
        keys = both(lin, start, pair_cols(1, head))
        return jnp.where(in_head(head, rows), keys, code + ones_row(head, rows))

    def vals_of(start, head):
        vals = both(lin, start, pair_cols(2, head))
        return jnp.where(in_head(head, rows), vals, ones_row(head, rows))

    def queries_of(start):
        level, delta = spread_stats(both(pay, start, slice(WIDE, WIDE + LANES)))
        return query_codes(fq, start, level), delta

    def per_tile(tile, carry):
        here = slot_start(tile + tiles)
        codes, delta = queries_of(here)
        code_a = both(fk, here, slice(0, LANES))
        for head in range(GROUP):
            mine = in_head(head, rows)
            qa[head] = jnp.where(mine, both(lin, here, pair_cols(0, head)), codes)
            da[head] = jnp.where(mine, both(pay, here, pair_cols(0, head)), delta)
            ka[head] = keys_of(here, code_a, head)
            va[head] = vals_of(here, head)
            acc_q[head] = jnp.zeros((rows, LANES), F32)
        low, high = rng[2 * tile], rng[2 * tile + 1]

        def own_step(other, inner):
            start = slot_start(other)
            at = other - tiles
            code = both(fk, start, slice(0, LANES))

            def begin(head):
                keys = keys_of(start, code, head)
                return keys, dot_nt(qa[head], keys), dot_nt(da[head], vals_of(start, head))

            def finish(head, state):
                keys, scores, d_probs = state
                probs = jnp.exp(scores)
                d_scores = (probs * d_probs).astype(BF)
                acc_q[head] += dot_nn(d_scores, keys)
                acc_k[at, head] += dot_tn(d_scores, qa[head])
                acc_v[at, head] += dot_tn(probs.astype(BF), da[head])

            staged(range(GROUP), begin, finish)
            return inner

        lax.fori_loop(jnp.maximum(low, tiles), jnp.minimum(high, 2 * tiles), own_step, 0)
        before = jnp.maximum(jnp.minimum(high, tiles) - low, 0)
        upper = jnp.maximum(low, 2 * tiles)
        after = jnp.maximum(high - upper, 0)

        def far_step(index, inner):
            other = jnp.where(index < before, low + index, upper + index - before)
            start = slot_start(other)
            code = both(fk, start, slice(0, LANES))
            codes_b, delta_b = queries_of(start)

            def begin(item):
                head, side = item
                if side == 0:
                    keys = keys_of(start, code, head)
                    return keys, dot_nt(qa[head], keys), dot_nt(da[head], vals_of(start, head))
                mine = in_head(head, rows)
                query = jnp.where(mine, both(lin, start, pair_cols(0, head)), codes_b)
                d_ctx = jnp.where(mine, both(pay, start, pair_cols(0, head)), delta_b)
                return (query, d_ctx), dot_nt(ka[head], query), dot_nt(va[head], d_ctx)

            def finish(item, state):
                head, side = item
                operand, scores, d_probs = state
                probs = jnp.exp(scores)
                d_scores = (probs * d_probs).astype(BF)
                if side == 0:
                    acc_q[head] += dot_nn(d_scores, operand)
                else:
                    query, d_ctx = operand
                    acc_k[tile, head] += dot_nn(d_scores, query)
                    acc_v[tile, head] += dot_nn(probs.astype(BF), d_ctx)

            staged([(head, side) for head in range(GROUP) for side in range(2)], begin, finish)
            return inner

        lax.fori_loop(0, before + after, far_step, 0)
        put(acc_q, None, slot_start(tile), 0, 1.0 / math.sqrt(HEAD_DIM))
        return carry

    def put(acc, tile, first, part, scale):
        lower = lanes_of(rows) < HEAD_DIM
        for pair in range(PAIRED):
            sides = [2 * pair, 2 * pair + 1]
            left, right = (acc[k] if tile is None else acc[tile, k] for k in sides)
            cells = jnp.where(lower, left, right) * scale
            cells = cells.astype(BF)
            cols = slice(part * WIDE + pair * LANES, part * WIDE + (pair + 1) * LANES)
            for seg in range(2):
                dlin_out[seg, pl.ds(first, SLOT_TILE), cols] = cells[
                    seg * SLOT_TILE : (seg + 1) * SLOT_TILE
                ]

    lax.fori_loop(0, tiles, per_tile, 0)

    def last(tile, carry):
        put(acc_k, tile, slot_start(tile), 1, 1.0)
        put(acc_v, tile, slot_start(tile), 2, 1.0)
        return carry

    lax.fori_loop(0, tiles, last, 0)


def attend_scratch():
    rows = 2 * SLOT_TILE
    return [
        pltpu.VMEM((GROUP, rows, LANES), BF),
        pltpu.VMEM((GROUP, rows, LANES), F32),
        pltpu.VMEM((GROUP, rows, LANES), F32),
    ]


def third(part, shape):
    lead = (0,) * (len(shape) - 2)
    block = shape[:-2] + (shape[-2] // 3, shape[-1])
    return pl.BlockSpec(block, lambda _: lead + (part, 0))


def attend_own(tok, weights, bias, fq, fk, rng):
    slots = tok.shape[1]
    tiles = slots // SLOT_TILE
    rows = 2 * SLOT_TILE
    shapes = [
        ((2, slots, 3 * WIDE), BF),
        ((tiles, GROUP, rows, LANES), F32),
        ((tiles, rows, LANES), F32),
    ]
    return pl.pallas_call(
        functools.partial(own_kernel, tiles),
        out_shape=tuple(jax.ShapeDtypeStruct(shape, kind) for shape, kind in shapes),
        grid=(1,),
        in_specs=[SMEM, whole(bias.shape), third(1, fq.shape), third(1, fk.shape)]
        + [whole(weights.shape), whole(tok.shape)],
        out_specs=tuple(whole(shape) for shape, _ in shapes),
        scratch_shapes=attend_scratch(),
        compiler_params=vmem(20),
        cost_estimate=cost(1, 1),
        name="attend_own",
    )(rng, bias, fq, fk, weights, tok)


def attend_far(before, after, own, weights, bias, fq, fk, rng):
    slots = before.shape[1]
    tiles = slots // SLOT_TILE
    shapes = [
        ((2, slots, WIDE), F32),
        ((2, slots, WIDE), BF),
        ((2, slots, LANES), BF),
        ((2, slots, 3 * WIDE), BF),
        ((2, slots, 3 * WIDE), BF),
    ]
    return pl.pallas_call(
        functools.partial(far_kernel, tiles),
        out_shape=tuple(jax.ShapeDtypeStruct(shape, kind) for shape, kind in shapes),
        grid=(1,),
        in_specs=[SMEM, whole(bias.shape), third(1, fq.shape), third(0, fk.shape)]
        + [third(2, fk.shape), whole(weights.shape), whole(before.shape), whole(after.shape)]
        + [whole((2, slots, WIDE)), whole(own[1].shape), whole(own[2].shape)],
        out_specs=tuple(whole(shape) for shape, _ in shapes[:3]) + (ANY, ANY),
        scratch_shapes=attend_scratch()
        + [
            pltpu.VMEM((2, slots, 3 * WIDE), BF),
            pltpu.VMEM((2, slots, 3 * WIDE), BF),
            pltpu.SemaphoreType.DMA((2 * tiles,)),
        ],
        compiler_params=vmem(32),
        cost_estimate=cost(4, 8),
        name="attend_far",
    )(rng, bias, fq, fk, fk, weights, before, after, *own)


def attend_back(lins, pays, fq, fk, rng):
    slots = pays[1].shape[1]
    tiles = slots // SLOT_TILE
    rows = 2 * SLOT_TILE
    return pl.pallas_call(
        functools.partial(backward_kernel, tiles),
        out_shape=jax.ShapeDtypeStruct((2, slots, 3 * WIDE), BF),
        grid=(1,),
        in_specs=[SMEM, whole(fq.shape), whole(fk.shape)] + [ANY] * 6,
        out_specs=whole((2, slots, 3 * WIDE)),
        scratch_shapes=[
            pltpu.VMEM((2, 3 * slots, 3 * WIDE), BF),
            pltpu.VMEM((2, 3 * slots, WIDE + LANES), BF),
            pltpu.VMEM((GROUP, rows, LANES), BF),
            pltpu.VMEM((GROUP, rows, LANES), BF),
            pltpu.VMEM((GROUP, rows, LANES), BF),
            pltpu.VMEM((GROUP, rows, LANES), BF),
            pltpu.VMEM((GROUP, rows, LANES), F32),
            pltpu.VMEM((tiles, GROUP, rows, LANES), F32),
            pltpu.VMEM((tiles, GROUP, rows, LANES), F32),
            pltpu.SemaphoreType.DMA((6,)),
        ],
        compiler_params=vmem(32),
        cost_estimate=cost(24, 12),
        name="attend_back",
    )(rng, fq, fk, *pays, *lins)


def payload(d_ctx, ctx, stat):
    slots = d_ctx.shape[1]
    return pl.pallas_call(
        delta_kernel,
        out_shape=jax.ShapeDtypeStruct((2, slots, WIDE + LANES), BF),
        grid=(1,),
        in_specs=[whole(d_ctx.shape), whole(ctx.shape), whole(stat.shape)],
        out_specs=whole((2, slots, WIDE + LANES)),
        compiler_params=vmem(10),
        cost_estimate=cost(0.5, 3),
        name="payload",
    )(d_ctx, ctx, stat)


def norm_forward(hidden):
    mean_val = jnp.mean(hidden, axis=-1, keepdims=True)
    centred = hidden - mean_val
    rate = lax.rsqrt(jnp.mean(centred * centred, axis=-1, keepdims=True) + EPS)
    return centred * rate, rate


def norm_backward(d_normal, normal, rate):
    return rate * (
        d_normal
        - jnp.mean(d_normal, axis=-1, keepdims=True)
        - normal * jnp.mean(d_normal * normal, axis=-1, keepdims=True)
    )


def normal_share(values):
    bell = jnp.exp(values * values * -0.5)
    t = 1.0 / (1.0 + (0.3275911 / math.sqrt(2.0)) * jnp.abs(values))
    poly = 0.5 * 1.061405429
    for term in (-1.453152027, 1.421413741, -0.284496736, 0.254829592):
        poly = poly * t + 0.5 * term
    beyond = poly * t * bell
    share = jnp.where(values < 0.0, beyond, 1.0 - beyond)
    return share, bell * (1.0 / math.sqrt(2.0 * math.pi))


def chain_kernel(
    tok, ctx_a, ctx_b, cot, wo_a, wo_b, vecs, up_from, up_bias, down_from,
    out, d_first_out, d_ctx_a, d_ctx_b, act_out, d_pre_out, normed_out, d_down_out, d_attn_out,
    sums, up_sums, slope, up, down, sems,
):
    hidden = up.shape[1]
    chunk = min(256, hidden)
    up_copy = pltpu.make_async_copy(up_from, up, sems.at[0])
    down_copy = pltpu.make_async_copy(down_from, down, sems.at[1])

    @pl.when(pl.program_id(0) == 0)
    def _():
        up_copy.start()
        down_copy.start()
        sums[...] = jnp.zeros_like(sums)
        up_sums[...] = jnp.zeros_like(up_sums)

    out_bias, gain_1, shift_1, down_bias, gain_2, shift_2 = (vecs[k : k + 1, :] for k in range(6))

    def tally(row, cells):
        sums[row : row + 1, :] += jnp.sum(cells, axis=0, keepdims=True)

    first = (
        tok[0, 0].astype(F32)
        + (dot_nn(ctx_a[...], wo_a[...]) + dot_nn(ctx_b[...], wo_b[...]))
        + out_bias
    )
    normal_1, rate_1 = norm_forward(first)
    normed = normal_1 * gain_1 + shift_1
    normed_r = normed.astype(BF)
    normed_out[...] = normed_r

    @pl.when(pl.program_id(0) == 0)
    def _():
        up_copy.wait()
        down_copy.wait()

    second = [normed + down_bias]

    def columns(part):
        return slice(part * chunk, (part + 1) * chunk)

    def begin_up(part):
        return dot_nn(normed_r, up[:, columns(part)])

    def finish_up(part, lin):
        cols = columns(part)
        pre = lin + up_bias[:, cols]
        share, bell = normal_share(pre)
        slope[:, cols] = share + pre * bell
        act_r = (pre * share).astype(BF)
        act_out[:, cols] = act_r
        second[0] = second[0] + dot_nn(act_r, down[cols, :])

    staged(range(hidden // chunk), begin_up, finish_up, 1)
    second = second[0]
    normal_2, rate_2 = norm_forward(second)
    out[...] = (normal_2 * gain_2 + shift_2).astype(BF)
    d_out = cot[0, 0].astype(F32)
    tally(4, d_out * normal_2)
    tally(5, d_out)
    d_second = norm_backward(d_out * gain_2, normal_2, rate_2)
    tally(3, d_second)
    d_down_r = d_second.astype(BF)
    d_down_out[...] = d_down_r
    d_normed = [d_second]

    def begin_down(part):
        return dot_nt(d_down_r, down[columns(part), :])

    def finish_down(part, d_act):
        cols = columns(part)
        d_pre_r = (d_act * slope[:, cols]).astype(BF)
        d_pre_out[:, cols] = d_pre_r
        up_sums[0:1, cols] += jnp.sum(d_pre_r.astype(F32), axis=0, keepdims=True)
        d_normed[0] = d_normed[0] + dot_nt(d_pre_r, up[:, cols])

    staged(range(hidden // chunk), begin_down, finish_down, 1)
    d_normed = d_normed[0]
    tally(1, d_normed * normal_1)
    tally(2, d_normed)
    d_first = norm_backward(d_normed * gain_1, normal_1, rate_1)
    tally(0, d_first)
    d_first_out[...] = d_first
    d_attn_r = d_first.astype(BF)
    d_attn_out[...] = d_attn_r
    d_ctx_a[...] = dot_nt(d_attn_r, wo_a[...]).astype(BF)
    d_ctx_b[...] = dot_nt(d_attn_r, wo_b[...]).astype(BF)


def chain(micro, tokens, ctx_a, ctx_b, cotangent, wo_a, wo_b, vecs, up, up_bias, down):
    slots, model = tokens.shape[2:]
    hidden = up.shape[1]
    rows = min(CHAIN_ROWS, slots)
    of_micro = pl.BlockSpec((1, 1, rows, model), lambda i: (micro, 0, i, 0))
    sizes = [
        (model, BF), (model, F32), (WIDE, BF), (WIDE, BF), (hidden, BF), (hidden, BF),
        (model, BF), (model, BF), (model, BF),
    ]
    return pl.pallas_call(
        chain_kernel,
        out_shape=tuple(jax.ShapeDtypeStruct((slots, cols), kind) for cols, kind in sizes)
        + (jax.ShapeDtypeStruct((8, model), F32), jax.ShapeDtypeStruct((8, hidden), F32)),
        grid=(slots // rows,),
        in_specs=[
            of_micro,
            row_block(rows, WIDE),
            row_block(rows, WIDE),
            of_micro,
            whole(wo_a.shape),
            whole(wo_b.shape),
            whole(vecs.shape),
            pl.BlockSpec(memory_space=pltpu.HBM),
            whole(up_bias.shape),
            pl.BlockSpec(memory_space=pltpu.HBM),
        ],
        out_specs=tuple(row_block(rows, cols) for cols, _ in sizes)
        + (whole((8, model)), whole((8, hidden))),
        scratch_shapes=[
            pltpu.VMEM((rows, hidden), F32),
            pltpu.VMEM(up.shape, BF),
            pltpu.VMEM(down.shape, BF),
            pltpu.SemaphoreType.DMA((2,)),
        ],
        compiler_params=vmem(28),
        cost_estimate=cost(6, 12),
        name="chain",
    )(tokens, ctx_a, ctx_b, cotangent, wo_a, wo_b, vecs, up, up_bias, down)


def weight_kernel(*refs):
    acts, d_downs, normeds, d_pres, d_attns, ctx_as, ctx_bs, sums, up_sums = (
        refs[2 * k : 2 * k + 2] for k in range(9)
    )
    seg, out = refs[18], refs[19]
    step = pl.program_id(0)
    width = out.shape[1]
    parts = up_sums[0].shape[1] // width

    def summed(lefts, rights):
        left = jnp.concatenate([item[...] for item in lefts], axis=0)
        return dot_tn(left, jnp.concatenate([item[...] for item in rights], axis=0)).astype(BF)

    @pl.when(step < parts)
    def _():
        out[...] = summed(acts, d_downs)

    @pl.when((step >= parts) & (step < 2 * parts))
    def _():
        out[...] = summed(normeds, d_pres)

    @pl.when((step == 2 * parts) & (seg[0] == 0))
    def _():
        out[:WIDE, :] = summed(ctx_as, d_attns)
        out[WIDE:, :] = summed(ctx_bs, d_attns)

    @pl.when((step == 2 * parts) & (seg[0] != 0))
    def _():
        out[:WIDE, :] = summed(ctx_bs, d_attns)
        out[WIDE:, :] = summed(ctx_as, d_attns)

    @pl.when(step == 2 * parts + 1)
    def _():
        wide = up_sums[0][0:1, :] + up_sums[1][0:1, :]
        cells = [sums[0][...] + sums[1][...]]
        cells += [wide[:, k * width : (k + 1) * width] for k in range(parts)]
        cells += [jnp.zeros((width - 8 - parts, width), F32)]
        out[...] = jnp.concatenate(cells, axis=0).astype(BF)


def weight_grads(groups, seg, model):
    flat = [item for group in groups for item in group]
    slots, hidden = groups[0][0].shape
    parts = hidden // model

    def fixed(item):
        return pl.BlockSpec(item.shape, lambda i: (0, 0))

    def column(first):
        return pl.BlockSpec((slots, model), lambda i: (0, jnp.clip(i - first, 0, parts - 1)))

    specs = [column(0)] * 2
    specs += [fixed(item) for item in groups[1] + groups[2]]
    specs += [column(parts)] * 2
    specs += [fixed(item) for group in groups[4:] for item in group]
    return pl.pallas_call(
        weight_kernel,
        out_shape=pltpu.HBM(((2 * parts + 1) * model + 16, model), BF),
        grid=(2 * parts + 2,),
        in_specs=specs + [SMEM],
        out_specs=row_block(model, model),
        compiler_params=vmem(24),
        cost_estimate=cost(1, 2),
        name="weight_grads",
    )(*flat, seg)


def unpack_kernel(parts, cells, down_out, up_out, out_out):
    step = pl.program_id(0)

    @pl.when(step < parts)
    def _():
        down_out[...] = cells[...].astype(F32)

    @pl.when((step >= parts) & (step < 2 * parts))
    def _():
        up_out[...] = cells[...].astype(F32)

    @pl.when(step == 2 * parts)
    def _():
        out_out[...] = cells[...].astype(F32)


def unpack(cells, hidden):
    model = cells.shape[1]
    parts = hidden // model
    block = (model, model)
    return pl.pallas_call(
        functools.partial(unpack_kernel, parts),
        out_shape=(
            jax.ShapeDtypeStruct((hidden, model), F32),
            jax.ShapeDtypeStruct((model, hidden), F32),
            jax.ShapeDtypeStruct((model, model), F32),
        ),
        grid=(2 * parts + 1,),
        in_specs=[pl.BlockSpec(block, lambda i: (i, 0))],
        out_specs=(
            pl.BlockSpec(block, lambda i: (jnp.minimum(i, parts - 1), 0)),
            pl.BlockSpec(block, lambda i: (0, jnp.clip(i - parts, 0, parts - 1))),
            pl.BlockSpec(block, lambda i: (0, 0)),
        ),
        compiler_params=vmem(12),
        cost_estimate=cost(0.1, 16),
        name="unpack",
    )(cells)


def qkv_weight_kernel(micros, *refs):
    joints, d_lins, out = refs[:micros], refs[micros : 2 * micros], refs[-1]
    slots, model = joints[0].shape[1:]
    total = jnp.zeros((model, WIDE), F32)
    sums = jnp.zeros((1, WIDE), F32)
    for m in range(micros):
        for seg in range(2):
            cells = d_lins[m][seg]
            total = total + dot_tn(joints[m][seg], cells)
            sums = sums + jnp.sum(cells.astype(F32), axis=0, keepdims=True)
    out[:model, :] = total.astype(BF)
    first = lax.broadcasted_iota(jnp.int32, (16, WIDE), 0) == 0
    out[model : model + 16, :] = jnp.where(first, sums, 0.0).astype(BF)
    if out.shape[0] > model + 16:
        out[model + 16 :, :] = jnp.zeros((out.shape[0] - model - 16, WIDE), BF)


def qkv_weight_grad(joints, d_lins, after, rows):
    slots, model = joints[0].shape[1:]
    return pl.pallas_call(
        functools.partial(qkv_weight_kernel, len(joints)),
        out_shape=jax.ShapeDtypeStruct((rows, 3 * WIDE), BF),
        grid=(3,),
        in_specs=[pl.BlockSpec((2, slots, model), lambda i: (0, 0, 0))] * len(joints)
        + [pl.BlockSpec((2, slots, WIDE), lambda i: (0, 0, i))] * len(joints)
        + [ANY],
        out_specs=pl.BlockSpec((rows, WIDE), lambda i: (0, i)),
        compiler_params=vmem(20),
        cost_estimate=cost(1.6, 4),
        name="qkv_weight_grad",
    )(*joints, *d_lins, after)


def finish_kernel(cells, *refs):
    micros = (len(refs) - 3) // 2
    near, far = refs[:micros], refs[micros : 2 * micros]
    out, small, token_out = refs[2 * micros :]
    rows = out.shape[0]
    for seg in range(2):
        for part in range(3):
            first = (2 * part + seg) * WIDE
            block = cells[seg, :rows, part * WIDE : (part + 1) * WIDE]
            out[:, first : first + WIDE] = block.astype(F32)
    edge = cells[:, rows : rows + 16, :].astype(F32)
    small[...] = jnp.concatenate(
        [edge[seg, :, part * WIDE : (part + 1) * WIDE] for part in (0, 2) for seg in range(2)],
        axis=1,
    )
    for m in range(micros):
        token_out[m, 0] = near[m][...] + far[m][...].astype(F32)


def finish(cells, near, far):
    slots, model = near[0].shape
    shapes = [
        ((model, 6 * WIDE), F32),
        ((16, 4 * WIDE), F32),
        ((len(near), 1, slots, model), F32),
    ]
    flat = [cells, *near, *far]
    return pl.pallas_call(
        finish_kernel,
        out_shape=tuple(jax.ShapeDtypeStruct(shape, kind) for shape, kind in shapes),
        grid=(1,),
        in_specs=[whole(item.shape) for item in flat],
        out_specs=tuple(whole(shape) for shape, _ in shapes),
        compiler_params=vmem(28),
        cost_estimate=cost(0.1, 12),
        name="finish",
    )(*flat)


def swapped(value):
    return lax.ppermute(value, "seg", [(0, 1), (1, 0)])


def shifted(value, by):
    size = lax.axis_size("seq")
    return lax.ppermute(
        value, "seq", [(i, i + by) for i in range(size) if 0 <= i + by < size]
    )


def flipped(value, bit):
    return lax.ppermute(value, "seq", [(i, i ^ bit) for i in range(lax.axis_size("seq"))])


def pick(value, index, axis):
    zero = jnp.int32(0)
    starts = [zero] * value.ndim
    starts[axis] = lax.convert_element_type(index, jnp.int32)
    sizes = list(value.shape)
    sizes[axis] = 1
    part = lax.dynamic_slice(value, starts, sizes)
    return lax.reshape(part, value.shape[:axis] + value.shape[axis + 1 :])


def stacked(pieces):
    return lax.concatenate([lax.expand_dims(piece, (0,)) for piece in pieces], 0)


def by_segment(mine, other, seg):
    return lax.select(seg == 0, stacked([mine, other]), stacked([other, mine]))


def bit_groups(size):
    bits = size.bit_length() - 1
    groups = [(k, 1) for k in range(min(bits, 2))]
    groups += [(k, min(2, bits - k)) for k in range(2, bits, 2)]
    return groups


def moved(value, seg_flip, seq_flip):
    size = lax.axis_size("seq")
    total = size * lax.axis_size("seg")
    pairs = [(i, i ^ (seg_flip * size + seq_flip)) for i in range(total)]
    return lax.ppermute(value, ("seg", "seq"), pairs)


def scatter_seq(cells, seq):
    for shift, count in bit_groups(lax.axis_size("seq")):
        own = lax.bitwise_and(lax.shift_right_logical(seq, jnp.int32(shift)), jnp.int32(2**count - 1))
        split = cells.reshape((-1, 2**count) + cells.shape[1:])
        total = pick(split, own, 1).astype(F32)
        for turn in range(1, 2**count):
            total = total + moved(pick(split, own ^ turn, 1), 0, turn << shift).astype(F32)
        cells = total.astype(BF)
    return cells


def merged(cells, first, second):
    order = [k for k in range(cells.ndim) if k != first]
    order.insert(second, first)
    shape = [cells.shape[k] for k in order]
    if cells.shape[order[second - 1]] > 1:
        cells = lax.transpose(cells, order)
    shape[second - 1 : second + 1] = [shape[second - 1] * shape[second]]
    return lax.reshape(cells, shape)


def in_order(pieces, own):
    bit = 1
    pieces = list(pieces)
    while bit < len(pieces):
        turned = lax.ne(lax.bitwise_and(own, jnp.int32(bit)), jnp.int32(0))
        pieces = [
            lax.select(turned, pieces[k ^ bit], pieces[k]) for k in range(len(pieces))
        ]
        bit *= 2
    return stacked(pieces)


def gather_all(cells, seg, seq):
    groups = bit_groups(lax.axis_size("seq"))[::-1]
    for at, (shift, count) in enumerate(groups):
        turns = [turn << shift for turn in range(2**count)]
        own = lax.bitwise_and(lax.shift_right_logical(seq, jnp.int32(shift)), jnp.int32(2**count - 1))
        if at == max(len(groups) - 2, 0):
            sides = [
                in_order([moved(cells, g, t) if g or t else cells for t in turns], own)
                for g in range(2)
            ]
            cells = merged(in_order(sides, seg), 1, 2)
        else:
            pieces = in_order([moved(cells, 0, t) if t else cells for t in turns], own)
            cells = merged(pieces, 0, cells.ndim - 2)
    return cells


def code_tables(lengths, base, slots, extent):
    spans = jnp.maximum(lengths[:, 0], lengths[:, 1])
    count = spans.shape[1]
    order = jnp.arange(count, dtype=jnp.int32)
    ends = jnp.sum(jnp.where(order[None, :] <= order[:, None], spans[:, None, :], 0), axis=2)
    place = base + jnp.arange(extent, dtype=jnp.int32)
    past = ends[:, None, :] <= place[None, :, None]
    pair = jnp.sum(past.astype(jnp.int32), axis=2)
    start = jnp.sum(jnp.where(past, spans[:, None, :], 0), axis=2)
    here = order[None, None, :] == pair[:, :, None]
    stop = jnp.sum(jnp.where(here, ends[:, None, :], 0), axis=2)
    inside = (pair < count) & (place >= 0)[None, :]
    counts = [jnp.sum(jnp.where(here, lengths[:, c, None, :], 0), axis=2) for c in range(2)]
    valid = jnp.stack(
        [inside & (place[None, :] - start < counts[c]) for c in range(2)], axis=1
    )
    lane = jnp.arange(LANES, dtype=jnp.int32) % HEAD_DIM
    digits = [pair, pair // DIGIT, pair // (DIGIT * DIGIT)]
    hot = jnp.zeros(pair.shape + (LANES,), bool)
    for k, digit in enumerate(digits):
        hot = hot | (lane == (digit % DIGIT)[:, :, None] + k * DIGIT)
    hot = hot & inside[:, :, None]
    is_code = lane <= BAD_LANE
    fq = jnp.where(is_code & ~hot, MASK_OFF, 0.0).astype(BF)
    bad = (lane == BAD_LANE) & ~valid[:, :, :, None]
    fk = (hot[:, None] | bad).astype(BF)
    low = jnp.where(inside, start, place[None, :])
    high = jnp.where(inside, stop, place[None, :])
    first = extent // 3
    low = jnp.clip(low[:, first : first + slots : SLOT_TILE] - base, 0, extent)
    last = first + SLOT_TILE - 1
    high = jnp.clip(high[:, last : first + slots : SLOT_TILE] - base, 0, extent)
    rng = jnp.stack([low // SLOT_TILE, -(-high // SLOT_TILE)], axis=2)
    return fq, fk, rng.reshape(rng.shape[0], -1).astype(jnp.int32)


def second_half(seg, seq, pays, forwards, owns, fq, fk, rng, joint, own_cols, d_firsts):
    micros = len(pays)
    ring = lax.axis_size("seq")
    slots, model = joint[0].shape[1:]
    d_lins, near, far = [], [], []
    pays = [*pays[:-1], (shifted(pays[-1], 1), pays[-1], shifted(pays[-1], -1))]
    for m in range(micros):
        lins = (forwards[m][3], owns[m][0], forwards[m][4])
        d_lin = attend_back(lins, pays[m], fq[m], fk[m], rng[m])
        d_lins.append(d_lin)
        far.append(swapped(dot_nt(pick(d_lin, 1 - seg, 0), own_cols).astype(BF)))
        near.append(d_firsts[m] + dot_nt(pick(d_lin, seg, 0), own_cols))
    late = model + 8 * max(ring, 16)
    qkv = qkv_weight_grad(joint, d_lins, far[0], late).reshape(ring, late // ring, 3 * WIDE)
    qkv = scatter_seq(qkv, seq)
    qkv, far[-1], near[-1] = lax.optimization_barrier((qkv, far[-1], near[-1]))
    qkv = gather_all(qkv, seg, seq).reshape(2, late, 3 * WIDE)
    qkv_grad, late_sums, token_grads = finish(qkv, near, far)
    return token_grads, qkv_grad, late_sums


def per_device(
    tokens,
    lengths,
    qkv_weight,
    query_bias,
    value_bias,
    out_weight,
    out_bias,
    attn_gain,
    attn_shift,
    up_weight,
    up_bias,
    down_weight,
    down_bias,
    ffn_gain,
    ffn_shift,
    cotangent,
):
    seg = lax.axis_index("seg")
    seq = lax.axis_index("seq")
    ring = lax.axis_size("seq")
    micros, _, slots, model = tokens.shape
    hidden = up_weight.shape[1]
    extent = 3 * slots
    mine = [tokens[m, 0] for m in range(micros)]
    joint = []
    partner = None
    for m in range(micros):
        sent = mine[m]
        if m:
            sent, partner = lax.optimization_barrier((sent, partner))
            joint[-1] = by_segment(mine[m - 1], partner, seg)
        partner = swapped(sent)
        joint.append(by_segment(sent, partner, seg))
    before, after = [], []
    fq, fk, rng = code_tables(lengths, seq * slots - slots, slots, extent)
    own_cols = pick(qkv_weight.reshape(model, 3, 2, WIDE), seg, 2).reshape(model, 3 * WIDE)
    own_bias = jnp.concatenate(
        [
            pick(query_bias.reshape(2, WIDE), seg, 0),
            jnp.zeros((WIDE,), query_bias.dtype),
            pick(value_bias.reshape(2, WIDE), seg, 0),
        ]
    ).astype(F32)
    own_bias = jnp.broadcast_to(own_bias, (8, 3 * WIDE))
    halves = out_weight.reshape(2, WIDE, model)
    wo_a, wo_b = pick(halves, seg, 0), pick(halves, 1 - seg, 0)
    vecs = jnp.stack(
        [out_bias, attn_gain, attn_shift, down_bias, ffn_gain, ffn_shift, out_bias, out_bias]
    ).astype(F32)
    up_row = up_bias.astype(F32)[None, :]
    before.append(shifted(joint[0], 1))
    after.append(shifted(joint[0], -1))
    owns = [attend_own(joint[m], own_cols, own_bias, fq[m], fk[m], rng[m]) for m in range(micros)]
    for m in range(1, micros):
        sent, before[-1], after[-1], owns = lax.optimization_barrier(
            (joint[m], before[-1], after[-1], owns)
        )
        before.append(shifted(sent, 1))
        after.append(shifted(sent, -1))
    forwards = [
        attend_far(before[m], after[m], owns[m], own_cols, own_bias, fq[m], fk[m], rng[m])
        for m in range(micros)
    ]
    chains, contexts = [], []
    for m in range(micros):
        ctx_r = forwards[m][1]
        contexts.append((pick(ctx_r, seg, 0), swapped(pick(ctx_r, 1 - seg, 0))))
    contexts[0], forwards = lax.optimization_barrier((contexts[0], forwards))
    for m in range(micros):
        chains.append(
            chain(
                m, tokens, *contexts[m], cotangent, wo_a, wo_b, vecs, up_weight, up_row, down_weight
            )
        )
    def paid(m, arrived):
        return payload(by_segment(chains[m][2], arrived, seg), forwards[m][0], forwards[m][2])

    arrived = [swapped(item[3]) for item in chains]
    pays = [paid(m, arrived[m]) for m in range(micros - 1)]
    columns = [[item[k] for item in chains] for k in range(len(chains[0]))]
    columns[4], pays = lax.optimization_barrier((columns[4], pays))
    grads = weight_grads(
        [columns[4], columns[7], columns[6], columns[5], columns[8]]
        + [[c[0] for c in contexts], [c[1] for c in contexts]]
        + [columns[9], columns[10]],
        jnp.reshape(seg, (1,)).astype(jnp.int32),
        model,
    )
    pays = [(shifted(pay, 1), pay, shifted(pay, -1)) for pay in pays]
    grads, late, pays = lax.optimization_barrier((grads, arrived[-1], pays))
    grads = lax.psum(grads, ("seg", "seq"))
    pays.append(paid(micros - 1, late))
    d_firsts = [item[1] for item in chains]
    given = (pays, forwards, owns, fq, fk, rng, joint, own_cols, d_firsts)

    def taken(given):
        return second_half(seg, seq, *given)

    def empty(given):
        shapes = jax.eval_shape(taken, given)
        return jax.tree.map(lambda item: jnp.zeros(item.shape, item.dtype), shapes)

    token_grads, qkv_grad, late_sums = lax.cond(lengths[0, 0, 0] >= 0, taken, empty, given)
    down_grad, up_grad, out_grad = unpack(grads, hidden)
    tail = grads[2 * hidden + model : 2 * hidden + model + 16].astype(F32)
    return (
        jnp.stack([item[0] for item in chains])[:, None],
        token_grads,
        qkv_grad,
        late_sums[0, :model],
        late_sums[0, model:],
        out_grad,
        tail[0],
        tail[1],
        tail[2],
        up_grad,
        tail[8 : 8 + hidden // model].reshape(-1),
        down_grad,
        tail[3],
        tail[4],
        tail[5],
    )


def solution(mesh):
    split = P(None, "seg", "seq", None)
    return jax.shard_map(
        per_device,
        mesh=mesh,
        in_specs=(split,) + (P(),) * 14 + (split,),
        out_specs=(split, split) + (P(),) * 13,
        check_vma=False,
    )
```

```python
import functools
import math

import jax
import jax.numpy as jnp
from jax import lax
from jax.experimental import pallas as pl
from jax.experimental.pallas import tpu as pltpu
from jax.sharding import PartitionSpec as P

HEADS = 8
HEAD_DIM = 64
LONGEST = 512
FLOOR_MAX = -10000.0
MASK_OFF = -1e30
EPS = 1e-12
LANES = 128
SLOT_TILE = 128
DIGIT = 13
DIGITS = 3
BAD_LANE = DIGIT * DIGITS
STAT_LANE = BAD_LANE + 1
GROUP = HEADS // 2
WIDE = GROUP * HEAD_DIM
PAIRED = WIDE // LANES
CHAIN_ROWS = 256
BF = jnp.bfloat16
F32 = jnp.float32
ANY = pl.BlockSpec(memory_space=pl.ANY)
SMEM = pl.BlockSpec(memory_space=pltpu.SMEM)


def whole(shape):
    zeros = (0,) * len(shape)
    return pl.BlockSpec(shape, lambda _: zeros)


def row_block(rows, cols):
    return pl.BlockSpec((rows, cols), lambda i: (i, 0))


def vmem(mega):
    return pltpu.CompilerParams(vmem_limit_bytes=mega * 1024 * 1024)


def cost(giga, mega):
    return pl.CostEstimate(
        flops=int(giga * 10**9), bytes_accessed=int(mega * 10**6), transcendentals=0
    )


def dot_nn(left, right):
    return lax.dot_general(left, right, (((1,), (0,)), ((), ())), preferred_element_type=F32)


def dot_nt(left, right):
    return lax.dot_general(left, right, (((1,), (1,)), ((), ())), preferred_element_type=F32)


def dot_tn(left, right):
    return lax.dot_general(left, right, (((0,), (0,)), ((), ())), preferred_element_type=F32)


def lanes_of(rows):
    return lax.broadcasted_iota(jnp.int32, (rows, LANES), 1)


def in_head(head, rows):
    lane = lanes_of(rows)
    return lane < HEAD_DIM if head % 2 == 0 else lane >= HEAD_DIM


def stat_lane(head):
    return STAT_LANE + 3 * head + (HEAD_DIM if head % 2 == 0 else 0)


def ones_row(head, rows):
    lane = lanes_of(rows)
    first = stat_lane(head)
    return ((lane >= first) & (lane < first + 3)).astype(F32).astype(BF)


def pair_cols(part, head):
    first = part * WIDE + (head // 2) * LANES
    return slice(first, first + LANES)


def both(ref, start, cols):
    return jnp.concatenate(
        [ref[seg, pl.ds(start, SLOT_TILE), cols] for seg in range(2)], axis=0
    )


def three_parts(values):
    high = values.astype(BF).astype(F32)
    rest = values - high
    mid = rest.astype(BF).astype(F32)
    low = (rest - mid).astype(BF).astype(F32)
    return high, mid, low


def copy_all(copies):
    for item in copies:
        item.start()
    for item in copies:
        item.wait()


def block_copies(blocks, scratch, sems, first):
    rows = scratch.shape[1] // 3
    return [
        pltpu.make_async_copy(
            block, scratch.at[:, pl.ds(at * rows, rows), :], sems.at[first + at]
        )
        for at, block in enumerate(blocks)
    ]


def slot_start(tile):
    return pl.multiple_of(tile * SLOT_TILE, SLOT_TILE)


def query_codes(fq, start, level=None):
    codes = fq[pl.ds(start, SLOT_TILE), :]
    codes = jnp.concatenate([codes, codes], axis=0)
    return codes if level is None else codes + level


def spread_stats(stats):
    wide = stats.astype(F32)
    rolled = pltpu.roll(wide, HEAD_DIM, 1)
    lower = lanes_of(stats.shape[0]) < HEAD_DIM
    level = jnp.where(lower, wide, rolled)
    delta = jnp.where(lower, rolled, wide)
    return level.astype(BF), delta.astype(BF)


def staged(items, begin, finish, ahead=2):
    held = []
    for item in items:
        held.append((item, begin(item)))
        if len(held) > ahead:
            finish(*held.pop(0))
    for entry in held:
        finish(*entry)


def projector(tok, lin, weights, bias):
    rows = 2 * SLOT_TILE

    def project(tile, carry):
        start = slot_start(tile)
        cells = dot_nn(both(tok, start, slice(0, tok.shape[2])), weights[...])
        cells = (cells + bias[0:1, :]).astype(BF)
        for part in range(3):
            cols = slice(part * WIDE, (part + 1) * WIDE)
            piece = cells[:, cols]
            if part == 0:
                piece = piece * (1.0 / math.sqrt(HEAD_DIM))
            for seg in range(2):
                lin[seg, pl.ds(start, SLOT_TILE), cols] = piece[
                    seg * SLOT_TILE : (seg + 1) * SLOT_TILE
                ]
        return carry

    return project


def make_queries(qa, lin, start, codes):
    rows = 2 * SLOT_TILE
    for head in range(GROUP):
        qa[head] = jnp.where(in_head(head, rows), both(lin, start, pair_cols(0, head)), codes)


def attend_step(qa, peak, acc, lin, start, code):
    rows = 2 * SLOT_TILE

    def begin(head):
        keys = both(lin, start, pair_cols(1, head))
        keys = jnp.where(in_head(head, rows), keys, code)
        return dot_nt(qa[head], keys)

    def finish(head, scores):
        vals = both(lin, start, pair_cols(2, head))
        vals = jnp.where(in_head(head, rows), vals, ones_row(head, rows))
        before = peak[head]
        top = jnp.maximum(before, jnp.max(scores, axis=1, keepdims=True))
        probs = jnp.exp(scores - jnp.concatenate([top] * (rows // LANES), axis=1))
        acc[head] = acc[head] * jnp.exp(before - top) + dot_nn(probs.astype(BF), vals)
        peak[head] = top

    staged(range(GROUP), begin, finish)


def head_lanes(lane, head):
    at = stat_lane(head)
    return (lane >= at) & (lane < at + 3)


def own_kernel(tiles, rng, bias, fq, fk, weights, tok, lin, acc_out, peak_out, qa, peak, acc):
    rows = 2 * SLOT_TILE
    lax.fori_loop(0, tiles, projector(tok, lin, weights, bias), 0)
    lane = lanes_of(rows)

    def per_tile(tile, carry):
        make_queries(qa, lin, slot_start(tile), query_codes(fq, slot_start(tile)))
        for head in range(GROUP):
            peak[head] = jnp.full((rows, LANES), FLOOR_MAX, F32)
            acc[head] = jnp.zeros((rows, LANES), F32)

        def step(other, inner):
            code = both(fk, slot_start(other), slice(0, LANES))
            attend_step(qa, peak, acc, lin, slot_start(other), code)
            return inner

        low = jnp.maximum(rng[2 * tile] - tiles, 0)
        high = jnp.minimum(rng[2 * tile + 1] - tiles, tiles)
        lax.fori_loop(low, high, step, 0)
        peaks = jnp.zeros((rows, LANES), F32)
        for head in range(GROUP):
            acc_out[tile, head] = acc[head]
            peaks = jnp.where(head_lanes(lane, head), peak[head], peaks)
        peak_out[tile] = peaks
        return carry

    lax.fori_loop(0, tiles, per_tile, 0)


def far_kernel(
    tiles, rng, bias, fq, fk_before, fk_after, weights, before, after, lin, acc_in, peak_in,
    ctx_out, ctx_r_out, stat_out, before_out, after_out, qa, peak, acc, lin_before, lin_after, sems,
):
    rows = 2 * SLOT_TILE
    lane = lanes_of(rows)
    reach = (
        (before, lin_before, before_out, jnp.minimum(rng[0], tiles), tiles, 0),
        (after, lin_after, after_out, 0, jnp.maximum(rng[2 * tiles - 1] - 2 * tiles, 0), tiles),
    )

    def kept(side, tile):
        _, scratch, out, _, _, base = side
        some = pl.ds(slot_start(tile), SLOT_TILE)
        return pltpu.make_async_copy(
            scratch.at[:, some, :], out.at[:, some, :], sems.at[base + tile]
        )

    for side in reach:
        project = projector(side[0], side[1], weights, bias)

        def fill(tile, carry, side=side, project=project):
            project(tile, carry)
            kept(side, tile).start()
            return carry

        lax.fori_loop(side[3], side[4], fill, 0)

    def per_tile(tile, carry):
        first = slot_start(tile)
        low, high = rng[2 * tile], rng[2 * tile + 1]
        end_before = jnp.minimum(high, tiles)
        start_after = jnp.maximum(low - 2 * tiles, 0)
        end_after = high - 2 * tiles
        for head in range(GROUP):
            acc[head] = acc_in[tile, head]
            at = stat_lane(head)
            peak[head] = jnp.broadcast_to(peak_in[tile][:, at : at + 1], (rows, LANES))

        @pl.when((low < end_before) | (start_after < end_after))
        def _():
            make_queries(qa, lin, first, query_codes(fq, first))

            def step_before(other, inner):
                code = both(fk_before, slot_start(other), slice(0, LANES))
                attend_step(qa, peak, acc, lin_before, slot_start(other), code)
                return inner

            def step_after(other, inner):
                code = both(fk_after, slot_start(other), slice(0, LANES))
                attend_step(qa, peak, acc, lin_after, slot_start(other), code)
                return inner

            lax.fori_loop(low, end_before, step_before, 0)
            lax.fori_loop(start_after, end_after, step_after, 0)

        totals = jnp.ones((rows, LANES), F32)
        peaks = jnp.zeros((rows, LANES), F32)
        for head in range(GROUP):
            mine = head_lanes(lane, head)
            totals = jnp.where(mine, acc[head], totals)
            peaks = jnp.where(mine, peak[head], peaks)
        totals = jnp.maximum(totals, 1.0)
        level = -(peaks + jnp.log(totals))
        level = jnp.where(lane < HEAD_DIM, level, 0.0) + pltpu.roll(
            jnp.where(lane < HEAD_DIM, 0.0, level), HEAD_DIM, 1
        )
        high_part, mid_part, low_part = three_parts(level)
        turn = (lane - STAT_LANE) % 3
        stats = jnp.where(turn == 0, high_part, jnp.where(turn == 1, mid_part, low_part))
        stats = stats.astype(BF)
        inverse = 1.0 / totals
        for pair in range(PAIRED):
            left, right = (
                acc[head] * inverse[:, stat_lane(head) : stat_lane(head) + 1]
                for head in (2 * pair, 2 * pair + 1)
            )
            cells = jnp.where(lane < HEAD_DIM, left, right)
            cols = slice(pair * LANES, (pair + 1) * LANES)
            for seg in range(2):
                part = cells[seg * SLOT_TILE : (seg + 1) * SLOT_TILE]
                ctx_out[seg, pl.ds(first, SLOT_TILE), cols] = part
                ctx_r_out[seg, pl.ds(first, SLOT_TILE), cols] = part.astype(BF)
        for seg in range(2):
            stat_out[seg, pl.ds(first, SLOT_TILE), :] = stats[seg * SLOT_TILE : (seg + 1) * SLOT_TILE]
        return carry

    lax.fori_loop(0, tiles, per_tile, 0)
    for side in reach:

        def settle(tile, carry, side=side):
            kept(side, tile).wait()
            return carry

        lax.fori_loop(side[3], side[4], settle, 0)


def delta_kernel(d_ctx, ctx, stat, pay_out):
    rows = d_ctx.shape[1]
    lane = lanes_of(rows)
    for seg in range(2):
        stats = stat[seg].astype(F32)
        for pair in range(PAIRED):
            cols = slice(pair * LANES, (pair + 1) * LANES)
            cells = d_ctx[seg, :, cols]
            pay_out[seg, :, cols] = cells
            product = cells.astype(F32) * ctx[seg, :, cols]
            for half in range(2):
                head = 2 * pair + half
                keep = lane < HEAD_DIM if half == 0 else lane >= HEAD_DIM
                delta = -jnp.sum(jnp.where(keep, product, 0.0), axis=1, keepdims=True)
                for k, part in enumerate(three_parts(delta)):
                    at = HEAD_DIM + STAT_LANE + 3 * head + k
                    stats = jnp.where(lane == at, part, stats)
        pay_out[seg, :, WIDE : WIDE + LANES] = stats.astype(BF)


def backward_kernel(tiles, rng, fq, fk, *rest):
    pays, lins = rest[:3], rest[3:6]
    dlin_out, lin, pay, qa, da, ka, va, acc_q, acc_k, acc_v, sems = rest[6:]
    rows = 2 * SLOT_TILE
    copy_all(block_copies(pays, pay, sems, 0) + block_copies(lins, lin, sems, 3))
    acc_k[...] = jnp.zeros_like(acc_k)
    acc_v[...] = jnp.zeros_like(acc_v)

    def keys_of(start, code, head):
        keys = both(lin, start, pair_cols(1, head))
        return jnp.where(in_head(head, rows), keys, code + ones_row(head, rows))

    def vals_of(start, head):
        vals = both(lin, start, pair_cols(2, head))
        return jnp.where(in_head(head, rows), vals, ones_row(head, rows))

    def queries_of(start):
        level, delta = spread_stats(both(pay, start, slice(WIDE, WIDE + LANES)))
        return query_codes(fq, start, level), delta

    def per_tile(tile, carry):
        here = slot_start(tile + tiles)
        codes, delta = queries_of(here)
        code_a = both(fk, here, slice(0, LANES))
        for head in range(GROUP):
            mine = in_head(head, rows)
            qa[head] = jnp.where(mine, both(lin, here, pair_cols(0, head)), codes)
            da[head] = jnp.where(mine, both(pay, here, pair_cols(0, head)), delta)
            ka[head] = keys_of(here, code_a, head)
            va[head] = vals_of(here, head)
            acc_q[head] = jnp.zeros((rows, LANES), F32)
        low, high = rng[2 * tile], rng[2 * tile + 1]

        def own_step(other, inner):
            start = slot_start(other)
            at = other - tiles
            code = both(fk, start, slice(0, LANES))

            def begin(head):
                keys = keys_of(start, code, head)
                return keys, dot_nt(qa[head], keys), dot_nt(da[head], vals_of(start, head))

            def finish(head, state):
                keys, scores, d_probs = state
                probs = jnp.exp(scores)
                d_scores = (probs * d_probs).astype(BF)
                acc_q[head] += dot_nn(d_scores, keys)
                acc_k[at, head] += dot_tn(d_scores, qa[head])
                acc_v[at, head] += dot_tn(probs.astype(BF), da[head])

            staged(range(GROUP), begin, finish)
            return inner

        lax.fori_loop(jnp.maximum(low, tiles), jnp.minimum(high, 2 * tiles), own_step, 0)
        before = jnp.maximum(jnp.minimum(high, tiles) - low, 0)
        upper = jnp.maximum(low, 2 * tiles)
        after = jnp.maximum(high - upper, 0)

        def far_step(index, inner):
            other = jnp.where(index < before, low + index, upper + index - before)
            start = slot_start(other)
            code = both(fk, start, slice(0, LANES))
            codes_b, delta_b = queries_of(start)

            def begin(item):
                head, side = item
                if side == 0:
                    keys = keys_of(start, code, head)
                    return keys, dot_nt(qa[head], keys), dot_nt(da[head], vals_of(start, head))
                mine = in_head(head, rows)
                query = jnp.where(mine, both(lin, start, pair_cols(0, head)), codes_b)
                d_ctx = jnp.where(mine, both(pay, start, pair_cols(0, head)), delta_b)
                return (query, d_ctx), dot_nt(ka[head], query), dot_nt(va[head], d_ctx)

            def finish(item, state):
                head, side = item
                operand, scores, d_probs = state
                probs = jnp.exp(scores)
                d_scores = (probs * d_probs).astype(BF)
                if side == 0:
                    acc_q[head] += dot_nn(d_scores, operand)
                else:
                    query, d_ctx = operand
                    acc_k[tile, head] += dot_nn(d_scores, query)
                    acc_v[tile, head] += dot_nn(probs.astype(BF), d_ctx)

            staged([(head, side) for head in range(GROUP) for side in range(2)], begin, finish)
            return inner

        lax.fori_loop(0, before + after, far_step, 0)
        put(acc_q, None, slot_start(tile), 0, 1.0 / math.sqrt(HEAD_DIM))
        return carry

    def put(acc, tile, first, part, scale):
        lower = lanes_of(rows) < HEAD_DIM
        for pair in range(PAIRED):
            sides = [2 * pair, 2 * pair + 1]
            left, right = (acc[k] if tile is None else acc[tile, k] for k in sides)
            cells = jnp.where(lower, left, right) * scale
            cells = cells.astype(BF)
            cols = slice(part * WIDE + pair * LANES, part * WIDE + (pair + 1) * LANES)
            for seg in range(2):
                dlin_out[seg, pl.ds(first, SLOT_TILE), cols] = cells[
                    seg * SLOT_TILE : (seg + 1) * SLOT_TILE
                ]

    lax.fori_loop(0, tiles, per_tile, 0)

    def last(tile, carry):
        put(acc_k, tile, slot_start(tile), 1, 1.0)
        put(acc_v, tile, slot_start(tile), 2, 1.0)
        return carry

    lax.fori_loop(0, tiles, last, 0)


def attend_scratch():
    rows = 2 * SLOT_TILE
    return [
        pltpu.VMEM((GROUP, rows, LANES), BF),
        pltpu.VMEM((GROUP, rows, LANES), F32),
        pltpu.VMEM((GROUP, rows, LANES), F32),
    ]


def third(part, shape):
    lead = (0,) * (len(shape) - 2)
    block = shape[:-2] + (shape[-2] // 3, shape[-1])
    return pl.BlockSpec(block, lambda _: lead + (part, 0))


def attend_own(tok, weights, bias, fq, fk, rng):
    slots = tok.shape[1]
    tiles = slots // SLOT_TILE
    rows = 2 * SLOT_TILE
    shapes = [
        ((2, slots, 3 * WIDE), BF),
        ((tiles, GROUP, rows, LANES), F32),
        ((tiles, rows, LANES), F32),
    ]
    return pl.pallas_call(
        functools.partial(own_kernel, tiles),
        out_shape=tuple(jax.ShapeDtypeStruct(shape, kind) for shape, kind in shapes),
        grid=(1,),
        in_specs=[SMEM, whole(bias.shape), third(1, fq.shape), third(1, fk.shape)]
        + [whole(weights.shape), whole(tok.shape)],
        out_specs=tuple(whole(shape) for shape, _ in shapes),
        scratch_shapes=attend_scratch(),
        compiler_params=vmem(20),
        cost_estimate=cost(1, 1),
        name="attend_own",
    )(rng, bias, fq, fk, weights, tok)


def attend_far(before, after, own, weights, bias, fq, fk, rng):
    slots = before.shape[1]
    tiles = slots // SLOT_TILE
    shapes = [
        ((2, slots, WIDE), F32),
        ((2, slots, WIDE), BF),
        ((2, slots, LANES), BF),
        ((2, slots, 3 * WIDE), BF),
        ((2, slots, 3 * WIDE), BF),
    ]
    return pl.pallas_call(
        functools.partial(far_kernel, tiles),
        out_shape=tuple(jax.ShapeDtypeStruct(shape, kind) for shape, kind in shapes),
        grid=(1,),
        in_specs=[SMEM, whole(bias.shape), third(1, fq.shape), third(0, fk.shape)]
        + [third(2, fk.shape), whole(weights.shape), whole(before.shape), whole(after.shape)]
        + [whole((2, slots, WIDE)), whole(own[1].shape), whole(own[2].shape)],
        out_specs=tuple(whole(shape) for shape, _ in shapes[:3]) + (ANY, ANY),
        scratch_shapes=attend_scratch()
        + [
            pltpu.VMEM((2, slots, 3 * WIDE), BF),
            pltpu.VMEM((2, slots, 3 * WIDE), BF),
            pltpu.SemaphoreType.DMA((2 * tiles,)),
        ],
        compiler_params=vmem(32),
        cost_estimate=cost(4, 8),
        name="attend_far",
    )(rng, bias, fq, fk, fk, weights, before, after, *own)


def attend_back(lins, pays, fq, fk, rng):
    slots = pays[1].shape[1]
    tiles = slots // SLOT_TILE
    rows = 2 * SLOT_TILE
    return pl.pallas_call(
        functools.partial(backward_kernel, tiles),
        out_shape=jax.ShapeDtypeStruct((2, slots, 3 * WIDE), BF),
        grid=(1,),
        in_specs=[SMEM, whole(fq.shape), whole(fk.shape)] + [ANY] * 6,
        out_specs=whole((2, slots, 3 * WIDE)),
        scratch_shapes=[
            pltpu.VMEM((2, 3 * slots, 3 * WIDE), BF),
            pltpu.VMEM((2, 3 * slots, WIDE + LANES), BF),
            pltpu.VMEM((GROUP, rows, LANES), BF),
            pltpu.VMEM((GROUP, rows, LANES), BF),
            pltpu.VMEM((GROUP, rows, LANES), BF),
            pltpu.VMEM((GROUP, rows, LANES), BF),
            pltpu.VMEM((GROUP, rows, LANES), F32),
            pltpu.VMEM((tiles, GROUP, rows, LANES), F32),
            pltpu.VMEM((tiles, GROUP, rows, LANES), F32),
            pltpu.SemaphoreType.DMA((6,)),
        ],
        compiler_params=vmem(32),
        cost_estimate=cost(24, 12),
        name="attend_back",
    )(rng, fq, fk, *pays, *lins)


def payload(d_ctx, ctx, stat):
    slots = d_ctx.shape[1]
    return pl.pallas_call(
        delta_kernel,
        out_shape=jax.ShapeDtypeStruct((2, slots, WIDE + LANES), BF),
        grid=(1,),
        in_specs=[whole(d_ctx.shape), whole(ctx.shape), whole(stat.shape)],
        out_specs=whole((2, slots, WIDE + LANES)),
        compiler_params=vmem(10),
        cost_estimate=cost(0.5, 3),
        name="payload",
    )(d_ctx, ctx, stat)


def norm_forward(hidden):
    mean_val = jnp.mean(hidden, axis=-1, keepdims=True)
    centred = hidden - mean_val
    rate = lax.rsqrt(jnp.mean(centred * centred, axis=-1, keepdims=True) + EPS)
    return centred * rate, rate


def norm_backward(d_normal, normal, rate):
    return rate * (
        d_normal
        - jnp.mean(d_normal, axis=-1, keepdims=True)
        - normal * jnp.mean(d_normal * normal, axis=-1, keepdims=True)
    )


def normal_share(values):
    bell = jnp.exp(values * values * -0.5)
    t = 1.0 / (1.0 + (0.3275911 / math.sqrt(2.0)) * jnp.abs(values))
    poly = 0.5 * 1.061405429
    for term in (-1.453152027, 1.421413741, -0.284496736, 0.254829592):
        poly = poly * t + 0.5 * term
    beyond = poly * t * bell
    share = jnp.where(values < 0.0, beyond, 1.0 - beyond)
    return share, bell * (1.0 / math.sqrt(2.0 * math.pi))


def chain_kernel(
    tok, ctx_a, ctx_b, cot, wo_a, wo_b, vecs, up_from, up_bias, down_from,
    out, d_first_out, d_ctx_a, d_ctx_b, act_out, d_pre_out, normed_out, d_down_out, d_attn_out,
    sums, up_sums, slope, up, down, sems,
):
    hidden = up.shape[1]
    chunk = min(256, hidden)
    up_copy = pltpu.make_async_copy(up_from, up, sems.at[0])
    down_copy = pltpu.make_async_copy(down_from, down, sems.at[1])

    @pl.when(pl.program_id(0) == 0)
    def _():
        up_copy.start()
        down_copy.start()
        sums[...] = jnp.zeros_like(sums)
        up_sums[...] = jnp.zeros_like(up_sums)

    out_bias, gain_1, shift_1, down_bias, gain_2, shift_2 = (vecs[k : k + 1, :] for k in range(6))

    def tally(row, cells):
        sums[row : row + 1, :] += jnp.sum(cells, axis=0, keepdims=True)

    first = (
        tok[0, 0].astype(F32)
        + (dot_nn(ctx_a[...], wo_a[...]) + dot_nn(ctx_b[...], wo_b[...]))
        + out_bias
    )
    normal_1, rate_1 = norm_forward(first)
    normed = normal_1 * gain_1 + shift_1
    normed_r = normed.astype(BF)
    normed_out[...] = normed_r

    @pl.when(pl.program_id(0) == 0)
    def _():
        up_copy.wait()
        down_copy.wait()

    second = [normed + down_bias]

    def columns(part):
        return slice(part * chunk, (part + 1) * chunk)

    def begin_up(part):
        return dot_nn(normed_r, up[:, columns(part)])

    def finish_up(part, lin):
        cols = columns(part)
        pre = lin + up_bias[:, cols]
        share, bell = normal_share(pre)
        slope[:, cols] = share + pre * bell
        act_r = (pre * share).astype(BF)
        act_out[:, cols] = act_r
        second[0] = second[0] + dot_nn(act_r, down[cols, :])

    staged(range(hidden // chunk), begin_up, finish_up, 1)
    second = second[0]
    normal_2, rate_2 = norm_forward(second)
    out[...] = (normal_2 * gain_2 + shift_2).astype(BF)
    d_out = cot[0, 0].astype(F32)
    tally(4, d_out * normal_2)
    tally(5, d_out)
    d_second = norm_backward(d_out * gain_2, normal_2, rate_2)
    tally(3, d_second)
    d_down_r = d_second.astype(BF)
    d_down_out[...] = d_down_r
    d_normed = [d_second]

    def begin_down(part):
        return dot_nt(d_down_r, down[columns(part), :])

    def finish_down(part, d_act):
        cols = columns(part)
        d_pre_r = (d_act * slope[:, cols]).astype(BF)
        d_pre_out[:, cols] = d_pre_r
        up_sums[0:1, cols] += jnp.sum(d_pre_r.astype(F32), axis=0, keepdims=True)
        d_normed[0] = d_normed[0] + dot_nt(d_pre_r, up[:, cols])

    staged(range(hidden // chunk), begin_down, finish_down, 1)
    d_normed = d_normed[0]
    tally(1, d_normed * normal_1)
    tally(2, d_normed)
    d_first = norm_backward(d_normed * gain_1, normal_1, rate_1)
    tally(0, d_first)
    d_first_out[...] = d_first
    d_attn_r = d_first.astype(BF)
    d_attn_out[...] = d_attn_r
    d_ctx_a[...] = dot_nt(d_attn_r, wo_a[...]).astype(BF)
    d_ctx_b[...] = dot_nt(d_attn_r, wo_b[...]).astype(BF)


def chain(micro, tokens, ctx_a, ctx_b, cotangent, wo_a, wo_b, vecs, up, up_bias, down):
    slots, model = tokens.shape[2:]
    hidden = up.shape[1]
    rows = min(CHAIN_ROWS, slots)
    of_micro = pl.BlockSpec((1, 1, rows, model), lambda i: (micro, 0, i, 0))
    sizes = [
        (model, BF), (model, F32), (WIDE, BF), (WIDE, BF), (hidden, BF), (hidden, BF),
        (model, BF), (model, BF), (model, BF),
    ]
    return pl.pallas_call(
        chain_kernel,
        out_shape=tuple(jax.ShapeDtypeStruct((slots, cols), kind) for cols, kind in sizes)
        + (jax.ShapeDtypeStruct((8, model), F32), jax.ShapeDtypeStruct((8, hidden), F32)),
        grid=(slots // rows,),
        in_specs=[
            of_micro,
            row_block(rows, WIDE),
            row_block(rows, WIDE),
            of_micro,
            whole(wo_a.shape),
            whole(wo_b.shape),
            whole(vecs.shape),
            pl.BlockSpec(memory_space=pltpu.HBM),
            whole(up_bias.shape),
            pl.BlockSpec(memory_space=pltpu.HBM),
        ],
        out_specs=tuple(row_block(rows, cols) for cols, _ in sizes)
        + (whole((8, model)), whole((8, hidden))),
        scratch_shapes=[
            pltpu.VMEM((rows, hidden), F32),
            pltpu.VMEM(up.shape, BF),
            pltpu.VMEM(down.shape, BF),
            pltpu.SemaphoreType.DMA((2,)),
        ],
        compiler_params=vmem(28),
        cost_estimate=cost(6, 12),
        name="chain",
    )(tokens, ctx_a, ctx_b, cotangent, wo_a, wo_b, vecs, up, up_bias, down)


def weight_kernel(*refs):
    acts, d_downs, normeds, d_pres, d_attns, ctx_as, ctx_bs, sums, up_sums = (
        refs[2 * k : 2 * k + 2] for k in range(9)
    )
    seg, out = refs[18], refs[19]
    step = pl.program_id(0)
    width = out.shape[1]
    parts = up_sums[0].shape[1] // width

    def summed(lefts, rights):
        left = jnp.concatenate([item[...] for item in lefts], axis=0)
        return dot_tn(left, jnp.concatenate([item[...] for item in rights], axis=0)).astype(BF)

    @pl.when(step < parts)
    def _():
        out[...] = summed(acts, d_downs)

    @pl.when((step >= parts) & (step < 2 * parts))
    def _():
        out[...] = summed(normeds, d_pres)

    @pl.when((step == 2 * parts) & (seg[0] == 0))
    def _():
        out[:WIDE, :] = summed(ctx_as, d_attns)
        out[WIDE:, :] = summed(ctx_bs, d_attns)

    @pl.when((step == 2 * parts) & (seg[0] != 0))
    def _():
        out[:WIDE, :] = summed(ctx_bs, d_attns)
        out[WIDE:, :] = summed(ctx_as, d_attns)

    @pl.when(step == 2 * parts + 1)
    def _():
        wide = up_sums[0][0:1, :] + up_sums[1][0:1, :]
        cells = [sums[0][...] + sums[1][...]]
        cells += [wide[:, k * width : (k + 1) * width] for k in range(parts)]
        cells += [jnp.zeros((width - 8 - parts, width), F32)]
        out[...] = jnp.concatenate(cells, axis=0).astype(BF)


def weight_grads(groups, seg, model):
    flat = [item for group in groups for item in group]
    slots, hidden = groups[0][0].shape
    parts = hidden // model

    def fixed(item):
        return pl.BlockSpec(item.shape, lambda i: (0, 0))

    def column(first):
        return pl.BlockSpec((slots, model), lambda i: (0, jnp.clip(i - first, 0, parts - 1)))

    specs = [column(0)] * 2
    specs += [fixed(item) for item in groups[1] + groups[2]]
    specs += [column(parts)] * 2
    specs += [fixed(item) for group in groups[4:] for item in group]
    return pl.pallas_call(
        weight_kernel,
        out_shape=pltpu.HBM(((2 * parts + 1) * model + 16, model), BF),
        grid=(2 * parts + 2,),
        in_specs=specs + [SMEM],
        out_specs=row_block(model, model),
        compiler_params=vmem(24),
        cost_estimate=cost(1, 2),
        name="weight_grads",
    )(*flat, seg)


def unpack_kernel(parts, cells, down_out, up_out, out_out):
    step = pl.program_id(0)

    @pl.when(step < parts)
    def _():
        down_out[...] = cells[...].astype(F32)

    @pl.when((step >= parts) & (step < 2 * parts))
    def _():
        up_out[...] = cells[...].astype(F32)

    @pl.when(step == 2 * parts)
    def _():
        out_out[...] = cells[...].astype(F32)


def unpack(cells, hidden):
    model = cells.shape[1]
    parts = hidden // model
    block = (model, model)
    return pl.pallas_call(
        functools.partial(unpack_kernel, parts),
        out_shape=(
            jax.ShapeDtypeStruct((hidden, model), F32),
            jax.ShapeDtypeStruct((model, hidden), F32),
            jax.ShapeDtypeStruct((model, model), F32),
        ),
        grid=(2 * parts + 1,),
        in_specs=[pl.BlockSpec(block, lambda i: (i, 0))],
        out_specs=(
            pl.BlockSpec(block, lambda i: (jnp.minimum(i, parts - 1), 0)),
            pl.BlockSpec(block, lambda i: (0, jnp.clip(i - parts, 0, parts - 1))),
            pl.BlockSpec(block, lambda i: (0, 0)),
        ),
        compiler_params=vmem(12),
        cost_estimate=cost(0.1, 16),
        name="unpack",
    )(cells)


def qkv_weight_kernel(micros, *refs):
    joints, d_lins, out = refs[:micros], refs[micros : 2 * micros], refs[-1]
    slots, model = joints[0].shape[1:]
    total = jnp.zeros((model, WIDE), F32)
    sums = jnp.zeros((1, WIDE), F32)
    for m in range(micros):
        for seg in range(2):
            cells = d_lins[m][seg]
            total = total + dot_tn(joints[m][seg], cells)
            sums = sums + jnp.sum(cells.astype(F32), axis=0, keepdims=True)
    out[:model, :] = total.astype(BF)
    first = lax.broadcasted_iota(jnp.int32, (16, WIDE), 0) == 0
    out[model : model + 16, :] = jnp.where(first, sums, 0.0).astype(BF)
    if out.shape[0] > model + 16:
        out[model + 16 :, :] = jnp.zeros((out.shape[0] - model - 16, WIDE), BF)


def qkv_weight_grad(joints, d_lins, after, rows):
    slots, model = joints[0].shape[1:]
    return pl.pallas_call(
        functools.partial(qkv_weight_kernel, len(joints)),
        out_shape=jax.ShapeDtypeStruct((rows, 3 * WIDE), BF),
        grid=(3,),
        in_specs=[pl.BlockSpec((2, slots, model), lambda i: (0, 0, 0))] * len(joints)
        + [pl.BlockSpec((2, slots, WIDE), lambda i: (0, 0, i))] * len(joints)
        + [ANY],
        out_specs=pl.BlockSpec((rows, WIDE), lambda i: (0, i)),
        compiler_params=vmem(20),
        cost_estimate=cost(1.6, 4),
        name="qkv_weight_grad",
    )(*joints, *d_lins, after)


def finish_kernel(cells, *refs):
    micros = (len(refs) - 3) // 2
    near, far = refs[:micros], refs[micros : 2 * micros]
    out, small, token_out = refs[2 * micros :]
    rows = out.shape[0]
    for seg in range(2):
        for part in range(3):
            first = (2 * part + seg) * WIDE
            block = cells[seg, :rows, part * WIDE : (part + 1) * WIDE]
            out[:, first : first + WIDE] = block.astype(F32)
    edge = cells[:, rows : rows + 16, :].astype(F32)
    small[...] = jnp.concatenate(
        [edge[seg, :, part * WIDE : (part + 1) * WIDE] for part in (0, 2) for seg in range(2)],
        axis=1,
    )
    for m in range(micros):
        token_out[m, 0] = near[m][...] + far[m][...].astype(F32)


def finish(cells, near, far):
    slots, model = near[0].shape
    shapes = [
        ((model, 6 * WIDE), F32),
        ((16, 4 * WIDE), F32),
        ((len(near), 1, slots, model), F32),
    ]
    flat = [cells, *near, *far]
    return pl.pallas_call(
        finish_kernel,
        out_shape=tuple(jax.ShapeDtypeStruct(shape, kind) for shape, kind in shapes),
        grid=(1,),
        in_specs=[whole(item.shape) for item in flat],
        out_specs=tuple(whole(shape) for shape, _ in shapes),
        compiler_params=vmem(28),
        cost_estimate=cost(0.1, 12),
        name="finish",
    )(*flat)


def swapped(value):
    return lax.ppermute(value, "seg", [(0, 1), (1, 0)])


def shifted(value, by):
    size = lax.axis_size("seq")
    return lax.ppermute(
        value, "seq", [(i, i + by) for i in range(size) if 0 <= i + by < size]
    )


def flipped(value, bit):
    return lax.ppermute(value, "seq", [(i, i ^ bit) for i in range(lax.axis_size("seq"))])


def pick(value, index, axis):
    zero = jnp.int32(0)
    starts = [zero] * value.ndim
    starts[axis] = lax.convert_element_type(index, jnp.int32)
    sizes = list(value.shape)
    sizes[axis] = 1
    part = lax.dynamic_slice(value, starts, sizes)
    return lax.reshape(part, value.shape[:axis] + value.shape[axis + 1 :])


def stacked(pieces):
    return lax.concatenate([lax.expand_dims(piece, (0,)) for piece in pieces], 0)


def by_segment(mine, other, seg):
    return lax.select(seg == 0, stacked([mine, other]), stacked([other, mine]))


def bit_groups(size):
    bits = size.bit_length() - 1
    groups = [(k, 1) for k in range(min(bits, 2))]
    groups += [(k, min(2, bits - k)) for k in range(2, bits, 2)]
    return groups


def moved(value, seg_flip, seq_flip):
    size = lax.axis_size("seq")
    total = size * lax.axis_size("seg")
    pairs = [(i, i ^ (seg_flip * size + seq_flip)) for i in range(total)]
    return lax.ppermute(value, ("seg", "seq"), pairs)


def scatter_seq(cells, seq):
    for shift, count in bit_groups(lax.axis_size("seq")):
        own = lax.bitwise_and(lax.shift_right_logical(seq, jnp.int32(shift)), jnp.int32(2**count - 1))
        split = cells.reshape((-1, 2**count) + cells.shape[1:])
        total = pick(split, own, 1).astype(F32)
        for turn in range(1, 2**count):
            total = total + moved(pick(split, own ^ turn, 1), 0, turn << shift).astype(F32)
        cells = total.astype(BF)
    return cells


def merged(cells, first, second):
    order = [k for k in range(cells.ndim) if k != first]
    order.insert(second, first)
    shape = [cells.shape[k] for k in order]
    if cells.shape[order[second - 1]] > 1:
        cells = lax.transpose(cells, order)
    shape[second - 1 : second + 1] = [shape[second - 1] * shape[second]]
    return lax.reshape(cells, shape)


def in_order(pieces, own):
    bit = 1
    pieces = list(pieces)
    while bit < len(pieces):
        turned = lax.ne(lax.bitwise_and(own, jnp.int32(bit)), jnp.int32(0))
        pieces = [
            lax.select(turned, pieces[k ^ bit], pieces[k]) for k in range(len(pieces))
        ]
        bit *= 2
    return stacked(pieces)


def gather_all(cells, seg, seq):
    groups = bit_groups(lax.axis_size("seq"))[::-1]
    for at, (shift, count) in enumerate(groups):
        turns = [turn << shift for turn in range(2**count)]
        own = lax.bitwise_and(lax.shift_right_logical(seq, jnp.int32(shift)), jnp.int32(2**count - 1))
        if at == max(len(groups) - 2, 0):
            sides = [
                in_order([moved(cells, g, t) if g or t else cells for t in turns], own)
                for g in range(2)
            ]
            cells = merged(in_order(sides, seg), 1, 2)
        else:
            pieces = in_order([moved(cells, 0, t) if t else cells for t in turns], own)
            cells = merged(pieces, 0, cells.ndim - 2)
    return cells


def code_tables(lengths, base, slots, extent):
    spans = jnp.maximum(lengths[:, 0], lengths[:, 1])
    count = spans.shape[1]
    order = jnp.arange(count, dtype=jnp.int32)
    ends = jnp.sum(jnp.where(order[None, :] <= order[:, None], spans[:, None, :], 0), axis=2)
    place = base + jnp.arange(extent, dtype=jnp.int32)
    past = ends[:, None, :] <= place[None, :, None]
    pair = jnp.sum(past.astype(jnp.int32), axis=2)
    start = jnp.sum(jnp.where(past, spans[:, None, :], 0), axis=2)
    here = order[None, None, :] == pair[:, :, None]
    stop = jnp.sum(jnp.where(here, ends[:, None, :], 0), axis=2)
    inside = (pair < count) & (place >= 0)[None, :]
    counts = [jnp.sum(jnp.where(here, lengths[:, c, None, :], 0), axis=2) for c in range(2)]
    valid = jnp.stack(
        [inside & (place[None, :] - start < counts[c]) for c in range(2)], axis=1
    )
    lane = jnp.arange(LANES, dtype=jnp.int32) % HEAD_DIM
    digits = [pair, pair // DIGIT, pair // (DIGIT * DIGIT)]
    hot = jnp.zeros(pair.shape + (LANES,), bool)
    for k, digit in enumerate(digits):
        hot = hot | (lane == (digit % DIGIT)[:, :, None] + k * DIGIT)
    hot = hot & inside[:, :, None]
    is_code = lane <= BAD_LANE
    fq = jnp.where(is_code & ~hot, MASK_OFF, 0.0).astype(BF)
    bad = (lane == BAD_LANE) & ~valid[:, :, :, None]
    fk = (hot[:, None] | bad).astype(BF)
    low = jnp.where(inside, start, place[None, :])
    high = jnp.where(inside, stop, place[None, :])
    first = extent // 3
    low = jnp.clip(low[:, first : first + slots : SLOT_TILE] - base, 0, extent)
    last = first + SLOT_TILE - 1
    high = jnp.clip(high[:, last : first + slots : SLOT_TILE] - base, 0, extent)
    rng = jnp.stack([low // SLOT_TILE, -(-high // SLOT_TILE)], axis=2)
    return fq, fk, rng.reshape(rng.shape[0], -1).astype(jnp.int32)


def second_half(seg, seq, pays, forwards, owns, fq, fk, rng, joint, own_cols, d_firsts):
    micros = len(pays)
    ring = lax.axis_size("seq")
    slots, model = joint[0].shape[1:]
    d_lins, near, far = [], [], []
    pays = [*pays[:-1], (shifted(pays[-1], 1), pays[-1], shifted(pays[-1], -1))]
    for m in range(micros):
        lins = (forwards[m][3], owns[m][0], forwards[m][4])
        d_lin = attend_back(lins, pays[m], fq[m], fk[m], rng[m])
        d_lins.append(d_lin)
        far.append(swapped(dot_nt(pick(d_lin, 1 - seg, 0), own_cols).astype(BF)))
        near.append(d_firsts[m] + dot_nt(pick(d_lin, seg, 0), own_cols))
    late = model + 8 * max(ring, 16)
    qkv = qkv_weight_grad(joint, d_lins, far[0], late).reshape(ring, late // ring, 3 * WIDE)
    qkv = scatter_seq(qkv, seq)
    qkv, far[-1], near[-1] = lax.optimization_barrier((qkv, far[-1], near[-1]))
    qkv = gather_all(qkv, seg, seq).reshape(2, late, 3 * WIDE)
    qkv_grad, late_sums, token_grads = finish(qkv, near, far)
    return token_grads, qkv_grad, late_sums


def per_device(
    tokens,
    lengths,
    qkv_weight,
    query_bias,
    value_bias,
    out_weight,
    out_bias,
    attn_gain,
    attn_shift,
    up_weight,
    up_bias,
    down_weight,
    down_bias,
    ffn_gain,
    ffn_shift,
    cotangent,
):
    seg = lax.axis_index("seg")
    seq = lax.axis_index("seq")
    ring = lax.axis_size("seq")
    micros, _, slots, model = tokens.shape
    hidden = up_weight.shape[1]
    extent = 3 * slots
    mine = [tokens[m, 0] for m in range(micros)]
    joint = []
    partner = None
    for m in range(micros):
        sent = mine[m]
        if m:
            sent, partner = lax.optimization_barrier((sent, partner))
            joint[-1] = by_segment(mine[m - 1], partner, seg)
        partner = swapped(sent)
        joint.append(by_segment(sent, partner, seg))
    before, after = [], []
    fq, fk, rng = code_tables(lengths, seq * slots - slots, slots, extent)
    own_cols = pick(qkv_weight.reshape(model, 3, 2, WIDE), seg, 2).reshape(model, 3 * WIDE)
    own_bias = jnp.concatenate(
        [
            pick(query_bias.reshape(2, WIDE), seg, 0),
            jnp.zeros((WIDE,), query_bias.dtype),
            pick(value_bias.reshape(2, WIDE), seg, 0),
        ]
    ).astype(F32)
    own_bias = jnp.broadcast_to(own_bias, (8, 3 * WIDE))
    halves = out_weight.reshape(2, WIDE, model)
    wo_a, wo_b = pick(halves, seg, 0), pick(halves, 1 - seg, 0)
    vecs = jnp.stack(
        [out_bias, attn_gain, attn_shift, down_bias, ffn_gain, ffn_shift, out_bias, out_bias]
    ).astype(F32)
    up_row = up_bias.astype(F32)[None, :]
    before.append(shifted(joint[0], 1))
    after.append(shifted(joint[0], -1))
    owns = [attend_own(joint[m], own_cols, own_bias, fq[m], fk[m], rng[m]) for m in range(micros)]
    for m in range(1, micros):
        sent, before[-1], after[-1], owns = lax.optimization_barrier(
            (joint[m], before[-1], after[-1], owns)
        )
        before.append(shifted(sent, 1))
        after.append(shifted(sent, -1))
    forwards = [
        attend_far(before[m], after[m], owns[m], own_cols, own_bias, fq[m], fk[m], rng[m])
        for m in range(micros)
    ]
    chains, contexts = [], []
    for m in range(micros):
        ctx_r = forwards[m][1]
        contexts.append((pick(ctx_r, seg, 0), swapped(pick(ctx_r, 1 - seg, 0))))
    contexts[0], forwards = lax.optimization_barrier((contexts[0], forwards))
    for m in range(micros):
        chains.append(
            chain(
                m, tokens, *contexts[m], cotangent, wo_a, wo_b, vecs, up_weight, up_row, down_weight
            )
        )
    def paid(m, arrived):
        return payload(by_segment(chains[m][2], arrived, seg), forwards[m][0], forwards[m][2])

    arrived = [swapped(item[3]) for item in chains[:-1]]
    arrived, sent = lax.optimization_barrier((arrived, chains[-1][3]))
    arrived.append(swapped(sent))
    pays = [paid(m, arrived[m]) for m in range(micros - 1)]
    columns = [[item[k] for item in chains] for k in range(len(chains[0]))]
    columns[4], pays = lax.optimization_barrier((columns[4], pays))
    grads = weight_grads(
        [columns[4], columns[7], columns[6], columns[5], columns[8]]
        + [[c[0] for c in contexts], [c[1] for c in contexts]]
        + [columns[9], columns[10]],
        jnp.reshape(seg, (1,)).astype(jnp.int32),
        model,
    )
    pays = [(shifted(pay, 1), pay, shifted(pay, -1)) for pay in pays]
    grads, late, pays = lax.optimization_barrier((grads, arrived[-1], pays))
    grads = lax.psum(grads, ("seg", "seq"))
    pays.append(paid(micros - 1, late))
    d_firsts = [item[1] for item in chains]
    given = (pays, forwards, owns, fq, fk, rng, joint, own_cols, d_firsts)

    def taken(given):
        return second_half(seg, seq, *given)

    def empty(given):
        shapes = jax.eval_shape(taken, given)
        return jax.tree.map(lambda item: jnp.zeros(item.shape, item.dtype), shapes)

    token_grads, qkv_grad, late_sums = lax.cond(lengths[0, 0, 0] >= 0, taken, empty, given)
    down_grad, up_grad, out_grad = unpack(grads, hidden)
    tail = grads[2 * hidden + model : 2 * hidden + model + 16].astype(F32)
    return (
        jnp.stack([item[0] for item in chains])[:, None],
        token_grads,
        qkv_grad,
        late_sums[0, :model],
        late_sums[0, model:],
        out_grad,
        tail[0],
        tail[1],
        tail[2],
        up_grad,
        tail[8 : 8 + hidden // model].reshape(-1),
        down_grad,
        tail[3],
        tail[4],
        tail[5],
    )


def solution(mesh):
    split = P(None, "seg", "seq", None)
    return jax.shard_map(
        per_device,
        mesh=mesh,
        in_specs=(split,) + (P(),) * 14 + (split,),
        out_specs=(split, split) + (P(),) * 13,
        check_vma=False,
    )
```
